128 devices in a mesh: gx: 8 (over x, core), gy: 16 (over z, y).
Axes of the slice: x: 4, y: 4, z: 4, core: 2. Of those that a mesh axis runs over, the one named last changes fastest.
Arguments:
- cell_local_coords: float32 [12288, 3, 128], P(('gx', 'gy')), may hold values from 0 to 1
- particle_speeds: float32 [12288, 3, 128], P(('gx', 'gy')), may hold values from -4 to 4
- thermal_state: float32 [12288, 128], P(('gx', 'gy')), may hold values from 0 to 2
- particle_weights: float32 [12288, 128], P(('gx', 'gy')), may hold values from 0.0018 to 0.0071
- boundary_flag: int32 [12288, 128], P(('gx', 'gy')), may hold values 0 or 1
- departing_local_groups: int32 [128, 2], P(('gx', 'gy')), may hold values from 0 to 95, as said below
- migrant_target_holder: int32 [128, 2], replicated, may hold values from 0 to 127, as said below
- target_entry_inputs: int32 [13312, 8], P(('gx', 'gy')), may hold values from 0 to 231
- adjacent_cell_label: int32 [13312, 4], P(('gx', 'gy')), may hold values from 0 to 25
Outputs:
- density: float32 [13312, 128], P(('gx', 'gy'))
- acceleration: float32 [13312, 3, 128], P(('gx', 'gy'))
- heating: float32 [13312, 128], P(('gx', 'gy'))
The draws below stay inside these ranges and needn't reach their ends.
Inputs may be any that keep to these rules, and one draw needn't show every extreme that they name: `departing_local_groups`: each row holds 2 different own block numbers of that owner. `migrant_target_holder`: an owner number for each crossing block; no owner receives more than 8 crossing blocks, and some owner receives exactly 8.
All inputs are finite; a program needn't handle non-finite values. No bound on the sum of `boundary_flag` on one device may be relied on, other than what follows from the above.
Results may differ from the reference program's by a relative error of at most 0.0003.
Values sent between devices are 32-bit elements; how exact they have to be, the bound alone decides.
No kernel may reach another device: no remote copies, remote signals or barrier semaphores. Data moves between devices by JAX's collectives and lax.ppermute only.
A program may use at most 64 MiB of HBM per device.

```python
import math
import jax
import jax.numpy as jnp
from jax import lax

GROUP_MEMBERS = 128
NB = 96
MIG = 2
IN_CAP = 8
SAME = 4
FACE = 4
BND = 16
SLOTS = 104
SOURCES = 232
LOCAL_GROUPS = 12288
TARGETS = 13312
N_GX = 8
N_GY = 16


def draw_departing_local_groups(key, part):
    key = jax.random.fold_in(key, 11)
    owners = N_GX * N_GY
    subkeys = jax.random.split(key, owners)
    return jax.vmap(lambda single: jax.random.permutation(single, NB)[:MIG])(subkeys).astype(jnp.int32)


def draw_migrant_target_holder(key, part):
    key = jax.random.fold_in(key, 23)
    owners = N_GX * N_GY
    first_key, second_key = jax.random.split(key)
    ranking = jax.random.permutation(first_key, owners)
    arrivals = jnp.where(ranking < owners // 8, IN_CAP, jnp.where(ranking < owners // 4, 2, 1)).astype(jnp.int32)
    listed = jnp.repeat(jnp.arange(owners).astype(jnp.int32), arrivals, total_repeat_length=owners * MIG)
    return jax.random.permutation(second_key, listed).reshape(owners, MIG).astype(jnp.int32)


def place_ends(values, key, smallest, high):
    place = [jax.random.randint(jax.random.fold_in(key, axis), (), 0, length) for axis, length in enumerate(values.shape)]
    widest = values.shape.index(max(values.shape))
    next_to = place[:widest] + [(place[widest] + 1) % values.shape[widest]] + place[widest + 1:]
    return values.at[tuple(place)].set(smallest).at[tuple(next_to)].set(high)


def block_scale(key, extent, cuts, low, top_value):
    level = 1.0
    for position, shards_of in cuts:
        heights = jax.random.uniform(jax.random.fold_in(jax.random.fold_in(key, 6), position), (shards_of,), jnp.float32, low / len(cuts), top_value / len(cuts))
        level = level * jnp.repeat(jnp.exp(heights), extent[position] // shards_of).reshape((-1,) + (1,) * (len(extent) - 1 - position))
    return level


def gaussian(own_key, shape, deviation, bound, shards=(), kind=jnp.bfloat16):
    level = block_scale(own_key, shape, shards, -0.22, 0.18) if shards else 1.0
    values = jax.random.normal(own_key, shape, jnp.float32) * deviation * level
    return jnp.minimum(jnp.maximum(values, -bound), bound).astype(kind)


def setup_inputs(seed: int = 0) -> dict:
    streams_of = jax.random.split(jax.random.key(seed), 10)
    cell_local_coords = jnp.clip(1.0 * jax.random.uniform(streams_of[0], (LOCAL_GROUPS, 3, GROUP_MEMBERS), jnp.float32) ** block_scale(streams_of[0], (LOCAL_GROUPS, 3, GROUP_MEMBERS), ((0, 128),), -0.2, 0.2), 0.0, 1.0)
    particle_speeds = gaussian(streams_of[1], (LOCAL_GROUPS, 3, GROUP_MEMBERS), 1.0, 4.0, ((0, 128),), jnp.float32)
    thermal_state = jnp.clip(2.0 * jax.random.uniform(streams_of[2], (LOCAL_GROUPS, GROUP_MEMBERS), jnp.float32) ** block_scale(streams_of[2], (LOCAL_GROUPS, GROUP_MEMBERS), ((0, 128),), -0.2, 0.2), 0.0, 2.0)
    particle_weights = jnp.clip(jnp.exp(math.log(0.0071) - 1.3723081 * jax.random.uniform(streams_of[3], (LOCAL_GROUPS, GROUP_MEMBERS), jnp.float32) ** block_scale(streams_of[3], (LOCAL_GROUPS, GROUP_MEMBERS), ((0, 128),), -0.2, 0.2)), 0.0018, 0.0071)
    boundary_flag = place_ends((jax.random.randint(streams_of[4], (LOCAL_GROUPS, GROUP_MEMBERS), 0, 4) < 1).astype(jnp.int32), jax.random.fold_in(streams_of[4], 1), 0, 1)
    departing_local_groups = draw_departing_local_groups(jax.random.fold_in(streams_of[9], 71), 0)
    migrant_target_holder = draw_migrant_target_holder(jax.random.fold_in(streams_of[9], 71), 0)
    target_entry_inputs = place_ends(jax.random.randint(streams_of[7], (TARGETS, SAME + FACE), 0, SOURCES), jax.random.fold_in(streams_of[7], 1), 0, SOURCES - 1).astype(jnp.int32)
    adjacent_cell_label = place_ends(jax.random.randint(streams_of[8], (TARGETS, FACE), 0, 26), jax.random.fold_in(streams_of[8], 1), 0, 25).astype(jnp.int32)
    return dict(cell_local_coords=cell_local_coords, particle_speeds=particle_speeds, thermal_state=thermal_state, particle_weights=particle_weights, boundary_flag=boundary_flag, departing_local_groups=departing_local_groups, migrant_target_holder=migrant_target_holder, target_entry_inputs=target_entry_inputs, adjacent_cell_label=adjacent_cell_label)


SMOOTH = 0.5
KERNEL = 21.0 / (16.0 * math.pi * SMOOTH ** 3)
REST = 1.0
BULK = 1.0
SOUND = math.sqrt(7.0 * BULK / REST)
VISC = 0.1
SOFT = 0.01 * SMOOTH ** 2
COND_FLUID = 1.0
COND_WALL = 4.0
GRAVITY = 1.0

def separation(target, sources, shifts):
    deltas = [target[:, None, axis_id, :, None] - sources[:, :, axis_id, None, :] - shifts[:, :, axis_id, None, None] for axis_id in range(3)]
    square = deltas[0] * deltas[0] + deltas[1] * deltas[1] + deltas[2] * deltas[2]
    spread = jnp.sqrt(square) / SMOOTH
    window = jnp.maximum(1.0 - 0.5 * spread, 0.0)
    return (deltas, square, spread, window)

def density_terms(target, sources, shifts):
    deltas, square, spread, window = separation(target, sources, shifts)
    weight = KERNEL * window ** 4 * (2.0 * spread + 1.0)
    return lax.optimization_barrier(jnp.sum(weight * sources[:, :, 7, None, :], axis=(1, 3)))

def safe_density(density_now, masses):
    return jnp.where(masses > 0.0, density_now, 1.0)

def pressure_term(density_now):
    return BULK * ((density_now / REST) ** 7 - 1.0) / (density_now * density_now)

def force_terms(target, sources, shifts, target_rho, source_rho):
    deltas, square, spread, window = separation(target, sources, shifts)
    slope = -5.0 * KERNEL / SMOOTH ** 2 * window ** 3
    closing = (target[:, None, 3, :, None] - sources[:, :, 3, None, :]) * deltas[0]
    closing = closing + (target[:, None, 4, :, None] - sources[:, :, 4, None, :]) * deltas[1]
    closing = closing + (target[:, None, 5, :, None] - sources[:, :, 5, None, :]) * deltas[2]
    approach = jnp.minimum(closing, 0.0) / (square + SOFT)
    mean_rho = 0.5 * (target_rho[:, None, :, None] + source_rho[:, :, None, :])
    viscous = -VISC * SOUND * SMOOTH * approach / mean_rho
    masses = sources[:, :, 7, None, :]
    coupling = masses * (pressure_term(target_rho)[:, None, :, None] + pressure_term(source_rho)[:, :, None, :] + viscous) * slope
    acceleration = jnp.stack([-lax.optimization_barrier(jnp.sum(coupling * deltas[axis_id], axis=(1, 3))) for axis_id in range(3)], 1)
    cond_target = (COND_FLUID + (COND_WALL - COND_FLUID) * target[:, 8])[:, None, :, None]
    cond_source = (COND_FLUID + (COND_WALL - COND_FLUID) * sources[:, :, 8])[:, :, None, :]
    pair_cond = 4.0 * cond_target * cond_source / (cond_target + cond_source)
    gap = target[:, None, 6, :, None] - sources[:, :, 6, None, :]
    product_rho = target_rho[:, None, :, None] * source_rho[:, :, None, :]
    heating = lax.optimization_barrier(jnp.sum(masses * pair_cond / product_rho * gap * slope * square / (square + SOFT), axis=(1, 3)))
    return (acceleration, heating)

def pair_lists(target_entry_inputs, adjacent_cell_label):
    own_rows = jnp.arange(target_entry_inputs.shape[0]).astype(jnp.int32)[:, None]
    indices = jnp.concatenate([own_rows, target_entry_inputs.astype(jnp.int32)], 1)
    codes = adjacent_cell_label + (adjacent_cell_label >= 13).astype(jnp.int32)
    steps_xyz = jnp.stack([codes // 9 - 1, codes // 3 % 3 - 1, codes % 3 - 1], -1).astype(jnp.float32)
    still = jnp.zeros((target_entry_inputs.shape[0], 1 + target_entry_inputs.shape[1] - adjacent_cell_label.shape[1], 3), jnp.float32)
    return (indices, jnp.concatenate([still, steps_xyz], 1))

def density_pass(blocks, source_table, indices, shifts):
    groups = blocks.shape[0] // 8

    def density_group(holding, inputs):
        target, rows, moves = inputs
        return (holding, density_terms(target, jnp.take(source_table, rows, axis=0), moves))
    unused, result = lax.scan(density_group, jnp.zeros((), jnp.float32), (blocks.reshape((groups, 8) + blocks.shape[1:]), indices.reshape(groups, 8, -1), shifts.reshape(groups, 8, -1, 3)))
    return result.reshape(blocks.shape[0], blocks.shape[2])

def force_pass(blocks, source_table, indices, shifts, density_now, rho_table):
    target_rho = safe_density(density_now, blocks[:, 7])
    table_rho = safe_density(rho_table, source_table[:, 7])
    groups = blocks.shape[0] // 8

    def force_group(holding, inputs):
        target, rows, moves, own_rho = inputs
        result = force_terms(target, jnp.take(source_table, rows, axis=0), moves, own_rho, jnp.take(table_rho, rows, axis=0))
        return (holding, result)
    unused, result = lax.scan(force_group, jnp.zeros((), jnp.float32), (blocks.reshape((groups, 8) + blocks.shape[1:]), indices.reshape(groups, 8, -1), shifts.reshape(groups, 8, -1, 3), target_rho.reshape(groups, 8, -1)))
    acceleration, heating = result
    return (acceleration.reshape(blocks.shape[0], 3, -1), heating.reshape(blocks.shape[0], -1))

def finish(blocks, density_now, acceleration, heating):
    living = blocks[:, 7] > 0.0
    fluid = 1.0 - blocks[:, 8]
    pull = jnp.array([0.0, 0.0, -GRAVITY], dtype=blocks.dtype)[None, :, None]
    moved = jnp.where(living[:, None, :], (acceleration + pull) * fluid[:, None, :], 0.0)
    return (jnp.where(living, density_now, 0.0), moved, jnp.where(living, heating, 0.0))

def arrivals(owner_id, dest_flat, leaving):
    total = dest_flat.shape[0]
    listing = jnp.arange(total).astype(jnp.int32)
    match = dest_flat == owner_id
    ranking = jnp.cumsum(match.astype(jnp.int32)) - 1
    slot_ids = jnp.arange(IN_CAP).astype(jnp.int32)
    taken = match[None, :] & (ranking[None, :] == slot_ids[:, None])
    wanted = lax.optimization_barrier(jnp.sum(jnp.where(taken, listing[None, :], 0), 1))
    present = jnp.any(taken, 1)
    return jnp.where(present[:, None, None], jnp.take(leaving, wanted, axis=0), 0.0)

def neighbours(exported):
    widths = [(1, 1), (1, 1)] + [(0, 0)] * (exported.ndim - 2)
    padded = jnp.pad(exported, widths)
    gathered = []
    for step_x in (-1, 0, 1):
        for step_y in (-1, 0, 1):
            if step_x != 0 or step_y != 0:
                gathered.append(padded[1 + step_x:1 + step_x + N_GX, 1 + step_y:1 + step_y + N_GY])
    stacked = jnp.stack(gathered, 2)
    return stacked.reshape((N_GX * N_GY, 8 * exported.shape[2]) + exported.shape[3:])

def device_outputs(device_items):
    blocks, source_table, indices, shifts, density_now, rho_table = device_items
    acceleration, heating = force_pass(blocks, source_table, indices, shifts, density_now, rho_table)
    return finish(blocks, density_now, acceleration, heating)

def reference(cell_local_coords, particle_speeds, thermal_state, particle_weights, boundary_flag, departing_local_groups, migrant_target_holder, target_entry_inputs, adjacent_cell_label):
    owners = N_GX * N_GY
    state_tables = jnp.concatenate([cell_local_coords, particle_speeds, thermal_state[:, None, :], particle_weights[:, None, :], boundary_flag.astype(cell_local_coords.dtype)[:, None, :]], 1)
    state_tables = state_tables.reshape((owners, NB) + state_tables.shape[1:])
    leaving = jax.vmap(lambda holding, chosen: jnp.take(holding, chosen, axis=0))(state_tables, departing_local_groups)
    leaving = leaving.reshape((owners * MIG,) + state_tables.shape[2:])
    dest_flat = migrant_target_holder.reshape(-1)
    arrived = jax.vmap(lambda owner_id: arrivals(owner_id, dest_flat, leaving))(jnp.arange(owners).astype(jnp.int32))
    numbers = jnp.arange(NB).astype(jnp.int32)
    departed = jnp.any(numbers[None, :, None] == departing_local_groups[:, None, :], 2)
    staying = jnp.where(departed[:, :, None, None], 0.0, state_tables)
    blocks = jnp.concatenate([arrived, staying], 1)
    ghosts = neighbours(blocks[:, :BND].reshape((N_GX, N_GY, BND) + blocks.shape[2:]))
    source_table = jnp.concatenate([blocks, ghosts], 1)
    indices, shifts = jax.vmap(pair_lists)(target_entry_inputs.reshape(owners, SLOTS, -1), adjacent_cell_label.reshape(owners, SLOTS, -1))
    density_now = lax.map(lambda device_items: density_pass(*device_items), (blocks, source_table, indices, shifts))
    ghost_rho = neighbours(density_now[:, :BND].reshape(N_GX, N_GY, BND, GROUP_MEMBERS))
    rho_table = jnp.concatenate([density_now, ghost_rho], 1)
    density_out, moved, heating = lax.map(device_outputs, (blocks, source_table, indices, shifts, density_now, rho_table))
    return (density_out.reshape(owners * SLOTS, GROUP_MEMBERS), moved.reshape(owners * SLOTS, 3, GROUP_MEMBERS), heating.reshape(owners * SLOTS, GROUP_MEMBERS))
```

```python
import functools
import math

import jax
import jax.numpy as jnp
import numpy as np
from jax import lax
from jax.experimental import pallas as pl
from jax.experimental.pallas import tpu as pltpu
from jax.sharding import PartitionSpec as P

IN_CAP = 8
BND = 16
SLOTS = 104
SOURCES = 232
LANES = 128
LINKS = 9

SMOOTH = 0.5
KERNEL = 21.0 / (16.0 * math.pi * SMOOTH**3)
SOUND = math.sqrt(7.0)
VISC = 0.1
SOFT = 0.01 * SMOOTH**2
GRAVITY = 1.0
KAPPA = -2.0 * VISC * SOUND * SMOOTH
SLOPE = 5.0 * KERNEL / SMOOTH**2
TINY = 1e-30

F32 = jnp.float32
BF16 = jnp.bfloat16

PARTS = ((0, 0), (0, 1), (0, 2), (1, 0), (1, 1), (2, 0))
ONE = 24


def place_rows(entries, rows):
    left = np.zeros((rows, 32), np.float32)
    right = np.zeros((rows, 32), np.float32)
    for at, ((ls, lrow), (rs, rrow)) in enumerate(entries):
        left[at, lrow] = ls
        right[at, rrow] = rs
    return left, right


def pair_rows():
    x, v, n, vx = (0, 1, 2), (3, 4, 5), 6, 7
    part = lambda p, channel: 8 * p + channel
    still, moved = [], []
    for k in range(3):
        still += [((-2, part(a, x[k])), (1, part(b, x[k]))) for a, b in PARTS]
    still += [((1, ONE), (1, part(p, n))) for p in range(3)]
    still += [((1, part(p, n)), (1, ONE)) for p in range(3)]
    weights = np.zeros((27, 64), np.float32)
    steps = np.array([(c // 9 - 1, c // 3 % 3 - 1, c % 3 - 1) for c in range(27)], np.float32)
    for k in range(3):
        for p in range(3):
            weights[:, len(moved)] = steps[:, k]
            moved.append(((-2, part(p, x[k])), (1, ONE)))
            weights[:, len(moved)] = steps[:, k]
            moved.append(((2, ONE), (1, part(p, x[k]))))
    weights[:, len(moved)] = (steps * steps).sum(1)
    moved.append(((1, ONE), (1, ONE)))
    c_still, c_moved = [], []
    c_still += [((1, part(p, vx)), (1, ONE)) for p in range(3)]
    c_still += [((1, ONE), (1, part(p, vx))) for p in range(3)]
    for k in range(3):
        c_still += [((-1, part(a, v[k])), (1, part(b, x[k]))) for a, b in PARTS]
        c_still += [((-1, part(a, x[k])), (1, part(b, v[k]))) for a, b in PARTS]
    for k in range(3):
        for p in range(3):
            weights[:, 32 + len(c_moved)] = steps[:, k]
            c_moved.append(((-1, part(p, v[k])), (1, ONE)))
            weights[:, 32 + len(c_moved)] = steps[:, k]
            c_moved.append(((1, ONE), (1, part(p, v[k]))))
    tables = [
        place_rows(still, 32), place_rows(moved, 32), place_rows(c_still, 48), place_rows(c_moved, 32)
    ]
    left = np.concatenate([t[0] for t in tables])
    right = np.concatenate([t[1] for t in tables])
    full = np.zeros((32, 64, LANES), np.float32)
    full[:27] = weights[:, :, None]
    shift = np.zeros((32, 8, LANES), np.float32)
    shift[:27, 3:6] = steps[:, :, None]
    return left, right, full, shift


def heat_rows():
    part = lambda p, channel: 8 * p + channel
    rows = [((1, part(a, 0)), (1, part(b, 3))) for a, b in PARTS]
    rows += [((1, part(a, 1)), (1, part(b, 4))) for a, b in PARTS]
    rows += [((-1, ONE), (1, part(p, 5))) for p in range(3)]
    rows += [((-1, part(0, 2)), (1, part(p, 6))) for p in range(3)]
    return place_rows(rows, 32)


def parts_of(block):
    high = block.astype(BF16)
    rest = block - high.astype(F32)
    middle = rest.astype(BF16)
    low = rest - middle.astype(F32)
    row = lax.broadcasted_iota(jnp.int32, block.shape, 0)
    ones = jnp.where(row == 0, 1.0, 0.0)
    return jnp.concatenate(
        [high.astype(F32), middle.astype(F32), low, ones], 0
    ).astype(BF16)


def channels(state, b):
    x = state[b, 0:3, :]
    v = state[b, 3:6, :] * KAPPA
    n = jnp.sum(x * x, 0, keepdims=True)
    vx = jnp.sum(x * v, 0, keepdims=True)
    return jnp.concatenate([x, v, n, vx], 0)


def dot(a, b, contract):
    return lax.dot_general(a, b, ((contract), ((), ())), preferred_element_type=F32)


def spread(place, parts, out, b, base):
    got = dot(place, parts, ((1,), (0,))).astype(BF16)
    for q in range(2):
        out[base + b + q] = got[:, LANES * q : LANES * (q + 1)]


def build_pairs(state, place_left, place_right, left, right):
    def both(b, carry):
        parts = jnp.concatenate([parts_of(channels(state, 2 * b + q)) for q in range(2)], 1)
        spread(place_left[...], parts, left, 2 * b, 0)
        spread(place_right[...], parts, right, 2 * b, 0)
        return carry

    def one(b, carry):
        parts = jnp.concatenate([parts_of(channels(state, 2 * b + q)) for q in range(2)], 1)
        spread(place_right[...], parts, right, 2 * b, 0)
        return carry

    lax.fori_loop(0, SLOTS // 2, both, 0)
    lax.fori_loop(SLOTS // 2, SOURCES // 2, one, 0)


GROUPS = ((0, 1), (2, 3), (4,), (5, 6), (7, 8))


def source_row(rows, t, k):
    return t if k == 0 else rows[t * 8 + k - 1]


def pair_products(t, rows, codes, left, right, weights, at, still, moved, wat, into):
    near = left[t, at : at + still, :]
    far = left[t, at : at + still + moved, :]
    for group in GROUPS:
        columns = []
        for k in group:
            row = source_row(rows, t, k)
            column = right[row, at : at + still, :]
            if k >= 5:
                extra = right[row, at + still : at + still + moved, :]
                code = codes[t * 4 + k - 5]
                extra = extra * weights[code, wat : wat + moved, :]
                column = jnp.concatenate([column, extra], 0)
            columns.append(column)
        sources = columns[0] if len(columns) == 1 else jnp.concatenate(columns, 1)
        made = dot(far if group[0] >= 5 else near, sources, ((0,), (0,)))
        into[:, LANES * group[0] : LANES * (group[-1] + 1)] = made


def paired_loop(stage, work, close):
    stage(0, 0)

    def step(u, carry):
        t = 2 * u
        stage(t + 1, 1)
        work(t, 0)
        close(jnp.maximum(t - 1, 0), 1)
        stage(jnp.minimum(t + 2, SLOTS - 1), 0)
        work(t + 1, 1)
        close(t, 0)
        return carry

    lax.fori_loop(0, SLOTS // 2, step, 0)
    close(SLOTS - 1, 1)


def density_kernel(rows, codes, state, place_left, place_right, weights, out, left, right, s0, s1, a0, a1):
    build_pairs(state, place_left, place_right, left, right)
    squares, sums = (s0, s1), (a0, a1)

    def stage(t, slot):
        pair_products(t, rows, codes, left, right, weights, 0, 32, 32, 0, squares[slot])

    def work(t, slot):
        square = squares[slot]
        masses = [state.at[source_row(rows, t, k)] for k in range(LINKS)]
        for o in range(16):
            total = None
            for k in range(LINKS):
                s = jnp.maximum(square[8 * o : 8 * o + 8, LANES * k : LANES * (k + 1)], TINY)
                w = jnp.maximum(1.0 - s * lax.rsqrt(s), 0.0)
                w2 = w * w
                term = (w2 * w2) * (1.25 - w) * masses[k][7:8, :]
                total = term if total is None else total + term
            sums[slot][8 * o : 8 * o + 8, :] = total

    def close(t, slot):
        rho = jnp.sum(sums[slot][...].T, 0, keepdims=True) * (4.0 * KERNEL)
        out[pl.ds(t, 1), :] = jnp.where(state[t, 7:8, :] > 0.0, rho, 0.0)

    paired_loop(stage, work, close)


def force_kernel(rows, codes, state, rho_table, place_left, place_right, heat_left, heat_right, weights, shift,
                 out_a, out_h, left, right, hleft, hright, per_source,
                 s0, s1, c0, c1, h0, h1, r0, r1, i0, i1, a0, a1):
    build_pairs(state, place_left, place_right, left, right)

    def build(b2, carry, both):
        mixed = []
        for q in range(2):
            b = 2 * b2 + q
            x, heat, mass, wall = state[b, 0:3, :], state[b, 6:7, :], state[b, 7:8, :], state[b, 8:9, :]
            rho = jnp.where(mass > 0.0, rho_table[pl.ds(b, 1), :], 1.0)
            inverse = 1.0 / rho
            r2 = rho * rho
            pressure = (r2 * r2 * r2 * rho - 1.0) * (inverse * inverse)
            zero = jnp.zeros_like(rho)
            per_source[b] = jnp.concatenate([rho, pressure, mass, mass * x, inverse, zero], 0)
            ratio = mass * inverse
            a = ratio * (2.0 + 1.2 * wall)
            bb = ratio * (1.2 + 3.6 * wall)
            mixed.append(parts_of(jnp.concatenate([heat, heat * wall, wall, a, bb, a * heat, bb * heat, zero], 0)))
        parts = jnp.concatenate(mixed, 1)
        if both:
            spread(heat_left[...], parts, hleft, 2 * b2, 0)
        spread(heat_right[...], parts, hright, 2 * b2, 0)
        return carry

    lax.fori_loop(0, SLOTS // 2, functools.partial(build, both=True), 0)
    lax.fori_loop(SLOTS // 2, SOURCES // 2, functools.partial(build, both=False), 0)
    squares, closings, heats, shifted, own, sums = (s0, s1), (c0, c1), (h0, h1), (r0, r1), (i0, i1), (a0, a1)

    def stage(t, slot):
        pair_products(t, rows, codes, left, right, weights, 0, 32, 32, 0, squares[slot])
        pair_products(t, rows, codes, left, right, weights, 64, 48, 32, 32, closings[slot])
        for group in GROUPS:
            columns = [hright[source_row(rows, t, k)] for k in group]
            sources = columns[0] if len(columns) == 1 else jnp.concatenate(columns, 1)
            heats[slot][:, LANES * group[0] : LANES * (group[-1] + 1)] = dot(hleft[t], sources, ((0,), (0,)))
        for f in range(4):
            row = source_row(rows, t, 5 + f)
            shifted[slot][f] = per_source[row] + shift[codes[t * 4 + f]] * per_source[row, 2:3, :]
        for at in range(2):
            own[slot][:, LANES * at : LANES * (at + 1)] = jnp.broadcast_to(per_source[t, at : at + 1, :], (LANES, LANES)).T

    def work(t, slot):
        views = [per_source.at[source_row(rows, t, k)] if k < 5 else shifted[slot].at[k - 5] for k in range(LINKS)]
        for o in range(16):
            eight = slice(8 * o, 8 * o + 8)
            rho_i = own[slot][eight, 0:LANES]
            p_i = own[slot][eight, LANES : 2 * LANES]
            totals = [None] * 5
            for k in range(LINKS):
                lanes = slice(LANES * k, LANES * (k + 1))
                view = views[k]
                s = jnp.maximum(squares[slot][eight, lanes], TINY)
                w = jnp.maximum(1.0 - s * lax.rsqrt(s), 0.0)
                w3 = w * w * w
                z = w3 * pl.reciprocal(s + SOFT, approx=True)
                viscous = jnp.maximum(closings[slot][eight, lanes], 0.0) * pl.reciprocal(rho_i + view[0:1, :], approx=True)
                coupling = (p_i + view[1:2, :]) * w3 + viscous * z
                terms = [coupling * view[2 + at : 3 + at, :] for at in range(4)]
                terms.append((s * z) * heats[slot][eight, lanes])
                totals = [term if total is None else total + term for total, term in zip(totals, terms)]
            for at in range(5):
                sums[slot][eight, LANES * at : LANES * (at + 1)] = totals[at]

    def close(t, slot):
        got = [jnp.sum(sums[slot][:, LANES * at : LANES * (at + 1)].T, 0, keepdims=True) for at in range(5)]
        living = state[t, 7:8, :] > 0.0
        fluid = 1.0 - state[t, 8:9, :]
        lines = []
        for k in range(3):
            push = SLOPE * (state[t, k : k + 1, :] * got[0] - got[1 + k])
            if k == 2:
                push = push - GRAVITY
            lines.append(jnp.where(living, push * fluid, 0.0))
        out_a[t] = jnp.concatenate(lines, 0)
        out_h[pl.ds(t, 1), :] = jnp.where(living, -SLOPE * got[4] * per_source[t, 6:7, :], 0.0)

    paired_loop(stage, work, close)


SMEM = pl.BlockSpec(memory_space=pltpu.SMEM)
VMEM = pl.BlockSpec(memory_space=pltpu.VMEM)


def density_call(rows, codes, state, place_left, place_right, weights):
    wide = (LANES, LINKS * LANES)
    return pl.pallas_call(
        density_kernel,
        out_shape=jax.ShapeDtypeStruct((SLOTS, LANES), F32),
        in_specs=[SMEM] * 2 + [VMEM] * 4,
        out_specs=VMEM,
        scratch_shapes=[
            pltpu.VMEM((SLOTS, 64, LANES), BF16),
            pltpu.VMEM((SOURCES, 64, LANES), BF16),
            pltpu.VMEM(wide, F32), pltpu.VMEM(wide, F32),
            pltpu.VMEM((LANES, LANES), F32), pltpu.VMEM((LANES, LANES), F32),
        ],
        compiler_params=pltpu.CompilerParams(vmem_limit_bytes=32 << 20),
        name="density_pass",
    )(rows, codes, state, place_left, place_right, weights)


def force_call(rows, codes, state, rho_table, place_left, place_right, heat_left, heat_right, weights, shift):
    wide = (LANES, LINKS * LANES)
    return pl.pallas_call(
        force_kernel,
        out_shape=(
            jax.ShapeDtypeStruct((SLOTS, 3, LANES), F32),
            jax.ShapeDtypeStruct((SLOTS, LANES), F32),
        ),
        in_specs=[SMEM] * 2 + [VMEM] * 8,
        out_specs=(VMEM, VMEM),
        scratch_shapes=[
            pltpu.VMEM((SLOTS, 144, LANES), BF16),
            pltpu.VMEM((SOURCES, 144, LANES), BF16),
            pltpu.VMEM((SLOTS, 32, LANES), BF16),
            pltpu.VMEM((SOURCES, 32, LANES), BF16),
            pltpu.VMEM((SOURCES, 8, LANES), F32),
        ]
        + [pltpu.VMEM(wide, F32)] * 6
        + [pltpu.VMEM((4, 8, LANES), F32)] * 2
        + [pltpu.VMEM((LANES, 2 * LANES), F32)] * 2
        + [pltpu.VMEM((LANES, 5 * LANES), F32)] * 2,
        compiler_params=pltpu.CompilerParams(vmem_limit_bytes=48 << 20),
        name="force_pass",
    )(rows, codes, state, rho_table, place_left, place_right, heat_left, heat_right, weights, shift)


def padded(shard, sides, width):
    for axis, dim in sides:
        size, length = (lax.axis_size(axis), shard.shape[dim])
        up = [(i, (i + 1) % size) for i in range(size - 1)]
        down = [(j, i) for i, j in up]
        last = lax.slice_in_dim(shard, length - width, length, axis=dim)
        first = lax.slice_in_dim(shard, 0, width, axis=dim)
        before = lax.ppermute(last, axis, up)
        after = lax.ppermute(first, axis, down)
        shard = jnp.concatenate([before, shard, after], axis=dim)
    return shard


def eight_around(haloed):
    flat = haloed.reshape((9,) + haloed.shape[2:])
    picked = jnp.concatenate([flat[:4], flat[5:]], 0)
    return picked.reshape((8 * haloed.shape[2],) + haloed.shape[3:])


def local(
    cell_local_coords,
    particle_speeds,
    thermal_state,
    particle_weights,
    boundary_flag,
    departing_local_groups,
    migrant_target_holder,
    target_entry_inputs,
    adjacent_cell_label,
):
    along = lax.axis_size("gy")
    myself = lax.axis_index("gx") * along + lax.axis_index("gy")
    state_tables = jnp.concatenate(
        [
            cell_local_coords,
            particle_speeds,
            thermal_state[:, None, :],
            particle_weights[:, None, :],
            boundary_flag.astype(jnp.float32)[:, None, :],
        ],
        1,
    )
    width = state_tables.shape[1]
    lanes = state_tables.shape[2]
    chosen = departing_local_groups[0]
    leaving = jnp.take(state_tables, chosen, axis=0)
    dest_flat = migrant_target_holder.reshape(-1)
    total = dest_flat.shape[0]
    listing = jnp.arange(total)
    match = dest_flat == myself
    ranking = jnp.cumsum(match.astype(jnp.int32)) - 1
    slot_ids = jnp.arange(IN_CAP)
    taken = match[None, :] & (ranking[None, :] == slot_ids[:, None])
    wanted = jnp.sum(jnp.where(taken, listing[None, :], 0), 1)
    present = jnp.any(taken, 1)
    incoming = lax.all_gather(leaving, ("gx", "gy"), axis=0, tiled=True)
    picked = jnp.take(incoming, wanted, axis=0)
    arrived = jnp.where(present[:, None, None], picked, 0.0)
    numbers = jnp.arange(state_tables.shape[0])
    departed = jnp.any(numbers[:, None] == chosen[None, :], 1)
    blocks = jnp.concatenate([arrived, jnp.where(departed[:, None, None], 0.0, state_tables)], 0)
    exported = blocks[:BND].reshape((1, 1, BND, width, lanes))
    haloed = padded(exported, (("gx", 0), ("gy", 1)), 1)
    state = jnp.concatenate([blocks, eight_around(haloed)], 0)
    rows = target_entry_inputs.reshape(-1)
    codes = (adjacent_cell_label + (adjacent_cell_label >= 13).astype(jnp.int32)).reshape(-1)
    left, right, weights, shift = pair_rows()
    heat_left, heat_right = heat_rows()
    left, right, weights, heat_left, heat_right = (
        jnp.asarray(a, BF16) for a in (left, right, weights, heat_left, heat_right)
    )
    shift = jnp.asarray(shift)
    density = density_call(rows, codes, state, left[:64], right[:64], weights)
    again = eight_around(
        padded(density[:BND].reshape((1, 1, BND, lanes)), (("gx", 0), ("gy", 1)), 1)
    )
    rho_table = jnp.concatenate([density, again], 0)
    acceleration, heating = force_call(
        rows, codes, state, rho_table, left, right, heat_left, heat_right, weights, shift
    )
    return density, acceleration, heating


def solution(mesh):
    return jax.shard_map(
        local,
        mesh=mesh,
        in_specs=(
            P(("gx", "gy"), None, None),
            P(("gx", "gy"), None, None),
            P(("gx", "gy"), None),
            P(("gx", "gy"), None),
            P(("gx", "gy"), None),
            P(("gx", "gy"), None),
            P(),
            P(("gx", "gy"), None),
            P(("gx", "gy"), None),
        ),
        out_specs=(P(("gx", "gy"), None), P(("gx", "gy"), None, None), P(("gx", "gy"), None)),
        check_vma=False,
    )
```

```python
import functools
import math

import jax
import jax.numpy as jnp
import numpy as np
from jax import lax
from jax.experimental import pallas as pl
from jax.experimental.pallas import tpu as pltpu
from jax.sharding import PartitionSpec as P

IN_CAP = 8
BND = 16
MIG = 2
N_GX = 8
N_GY = 16
SLOTS = 104
SOURCES = 232
LANES = 128
LINKS = 9

SMOOTH = 0.5
KERNEL = 21.0 / (16.0 * math.pi * SMOOTH**3)
SOUND = math.sqrt(7.0)
VISC = 0.1
SOFT = 0.01 * SMOOTH**2
GRAVITY = 1.0
KAPPA = -2.0 * VISC * SOUND * SMOOTH
SLOPE = 5.0 * KERNEL / SMOOTH**2
TINY = 1e-30

F32 = jnp.float32
BF16 = jnp.bfloat16

PARTS = ((0, 0), (0, 1), (0, 2), (1, 0), (1, 1), (2, 0))
ONE = 24


def place_rows(entries, rows):
    left = np.zeros((rows, 32), np.float32)
    right = np.zeros((rows, 32), np.float32)
    for at, ((ls, lrow), (rs, rrow)) in enumerate(entries):
        left[at, lrow] = ls
        right[at, rrow] = rs
    return left, right


def pair_rows():
    x, v, n, vx = (0, 1, 2), (3, 4, 5), 6, 7
    part = lambda p, channel: 8 * p + channel
    still, moved = [], []
    for k in range(3):
        still += [((-2, part(a, x[k])), (1, part(b, x[k]))) for a, b in PARTS]
    still += [((1, ONE), (1, part(p, n))) for p in range(3)]
    still += [((1, part(p, n)), (1, ONE)) for p in range(3)]
    weights = np.zeros((27, 64), np.float32)
    steps = np.array([(c // 9 - 1, c // 3 % 3 - 1, c % 3 - 1) for c in range(27)], np.float32)
    for k in range(3):
        for p in range(3):
            weights[:, len(moved)] = steps[:, k]
            moved.append(((-2, part(p, x[k])), (1, ONE)))
            weights[:, len(moved)] = steps[:, k]
            moved.append(((2, ONE), (1, part(p, x[k]))))
    weights[:, len(moved)] = (steps * steps).sum(1)
    moved.append(((1, ONE), (1, ONE)))
    c_still, c_moved = [], []
    c_still += [((1, part(p, vx)), (1, ONE)) for p in range(3)]
    c_still += [((1, ONE), (1, part(p, vx))) for p in range(3)]
    for k in range(3):
        c_still += [((-1, part(a, v[k])), (1, part(b, x[k]))) for a, b in PARTS]
        c_still += [((-1, part(a, x[k])), (1, part(b, v[k]))) for a, b in PARTS]
    for k in range(3):
        for p in range(3):
            weights[:, 32 + len(c_moved)] = steps[:, k]
            c_moved.append(((-1, part(p, v[k])), (1, ONE)))
            weights[:, 32 + len(c_moved)] = steps[:, k]
            c_moved.append(((1, ONE), (1, part(p, v[k]))))
    tables = [
        place_rows(still, 32), place_rows(moved, 32), place_rows(c_still, 48), place_rows(c_moved, 32)
    ]
    left = np.concatenate([t[0] for t in tables])
    right = np.concatenate([t[1] for t in tables])
    full = np.zeros((32, 64, LANES), np.float32)
    full[:27] = weights[:, :, None]
    shift = np.zeros((32, 8, LANES), np.float32)
    shift[:27, 3:6] = steps[:, :, None]
    return left, right, full, shift


def heat_rows():
    part = lambda p, channel: 8 * p + channel
    rows = [((1, part(a, 0)), (1, part(b, 3))) for a, b in PARTS]
    rows += [((1, part(a, 1)), (1, part(b, 4))) for a, b in PARTS]
    rows += [((-1, ONE), (1, part(p, 5))) for p in range(3)]
    rows += [((-1, part(0, 2)), (1, part(p, 6))) for p in range(3)]
    return place_rows(rows, 32)


def parts_of(block):
    high = block.astype(BF16)
    rest = block - high.astype(F32)
    middle = rest.astype(BF16)
    low = rest - middle.astype(F32)
    row = lax.broadcasted_iota(jnp.int32, block.shape, 0)
    ones = jnp.where(row == 0, 1.0, 0.0)
    return jnp.concatenate(
        [high.astype(F32), middle.astype(F32), low, ones], 0
    ).astype(BF16)


def channels(state, b):
    x = state[b, 0:3, :]
    v = state[b, 3:6, :] * KAPPA
    n = jnp.sum(x * x, 0, keepdims=True)
    vx = jnp.sum(x * v, 0, keepdims=True)
    return jnp.concatenate([x, v, n, vx], 0)


def dot(a, b, contract):
    return lax.dot_general(a, b, ((contract), ((), ())), preferred_element_type=F32)


UNROLL = 4


def twice(build):
    own, every = SLOTS // (2 * UNROLL), SOURCES // (2 * UNROLL)
    lax.fori_loop(0, own, functools.partial(build, both=True), 0)
    lax.fori_loop(own, every, functools.partial(build, both=False), 0)


def spread(place, parts, out, b):
    got = dot(place, parts, ((1,), (0,))).astype(BF16)
    for q in range(2):
        out[b + q] = got[:, LANES * q : LANES * (q + 1)]


def build_pairs(state, place_left, place_right, left, right):
    def build(b, carry, both):
        for u in range(UNROLL):
            at = 2 * (UNROLL * b + u)
            parts = jnp.concatenate([parts_of(channels(state, at + q)) for q in range(2)], 1)
            if both:
                spread(place_left[...], parts, left, at)
            spread(place_right[...], parts, right, at)
        return carry

    twice(build)


GROUPS = ((0, 1), (2, 3), (4,), (5, 6), (7, 8))


def source_row(rows, t, k):
    return t if k == 0 else rows[t * 8 + k - 1]


def pair_products(t, rows, codes, left, right, weights, at, still, moved, wat, into):
    near = left[t, at : at + still, :]
    far = left[t, at : at + still + moved, :]
    for group in GROUPS:
        columns = []
        for k in group:
            row = source_row(rows, t, k)
            column = right[row, at : at + still, :]
            if k >= 5:
                extra = right[row, at + still : at + still + moved, :]
                code = codes[t * 4 + k - 5]
                extra = extra * weights[code, wat : wat + moved, :]
                column = jnp.concatenate([column, extra], 0)
            columns.append(column)
        sources = columns[0] if len(columns) == 1 else jnp.concatenate(columns, 1)
        made = dot(far if group[0] >= 5 else near, sources, ((0,), (0,)))
        into[:, LANES * group[0] : LANES * (group[-1] + 1)] = made
        yield


def run(steps):
    for _ in steps:
        pass


def paired_loop(stage, work, close):
    run(stage(0, 0))

    def alternate(a, b):
        live = [a, b]
        while live:
            for g in list(live):
                if next(g, live) is live:
                    live.remove(g)

    def step(u, carry):
        t = 2 * u
        close(jnp.maximum(t - 1, 0), 1)
        alternate(work(t, 0), stage(t + 1, 1))
        close(t, 0)
        alternate(work(t + 1, 1), stage(jnp.minimum(t + 2, SLOTS - 1), 0))
        return carry

    lax.fori_loop(0, SLOTS // 2, step, 0)
    close(SLOTS - 1, 1)


def density_kernel(rows, codes, state, place_left, place_right, weights, out, left, right, s0, s1, a0, a1):
    build_pairs(state, place_left, place_right, left, right)
    squares, sums = (s0, s1), (a0, a1)

    def stage(t, slot):
        yield from pair_products(t, rows, codes, left, right, weights, 0, 32, 32, 0, squares[slot])

    def work(t, slot):
        square = squares[slot]
        masses = [state.at[source_row(rows, t, k)] for k in range(LINKS)]
        for o in range(16):
            total = None
            for k in range(LINKS):
                s = jnp.maximum(square[8 * o : 8 * o + 8, LANES * k : LANES * (k + 1)], TINY)
                w = jnp.maximum(1.0 - s * lax.rsqrt(s), 0.0)
                w2 = w * w
                term = (w2 * w2) * (1.25 - w) * masses[k][7:8, :]
                total = term if total is None else total + term
            sums[slot][8 * o : 8 * o + 8, :] = total
            yield

    def close(t, slot):
        rho = jnp.sum(sums[slot][...].T, 0, keepdims=True) * (4.0 * KERNEL)
        out[pl.ds(t, 1), :] = jnp.where(state[t, 7:8, :] > 0.0, rho, 0.0)

    paired_loop(stage, work, close)


def force_kernel(rows, codes, state, rho_table, place_left, place_right, heat_left, heat_right, weights, shift,
                 out_a, out_h, left, right, hleft, hright, per_source,
                 s0, s1, c0, c1, h0, h1, r0, r1, i0, i1, a0, a1):
    build_pairs(state, place_left, place_right, left, right)

    def heat_channels(b):
        x, heat, mass, wall = state[b, 0:3, :], state[b, 6:7, :], state[b, 7:8, :], state[b, 8:9, :]
        rho = jnp.where(mass > 0.0, rho_table[pl.ds(b, 1), :], 1.0)
        inverse = 1.0 / rho
        r2 = rho * rho
        pressure = (r2 * r2 * r2 * rho - 1.0) * (inverse * inverse)
        zero = jnp.zeros_like(rho)
        per_source[b] = jnp.concatenate([rho, pressure, mass, mass * x, inverse, zero], 0)
        ratio = mass * inverse
        a = ratio * (2.0 + 1.2 * wall)
        bb = ratio * (1.2 + 3.6 * wall)
        return jnp.concatenate([heat, heat * wall, wall, a, bb, a * heat, bb * heat, zero], 0)

    def build(b, carry, both):
        for u in range(UNROLL):
            at = 2 * (UNROLL * b + u)
            parts = jnp.concatenate([parts_of(heat_channels(at + q)) for q in range(2)], 1)
            if both:
                spread(heat_left[...], parts, hleft, at)
            spread(heat_right[...], parts, hright, at)
        return carry

    twice(build)
    squares, closings, heats, shifted, own, sums = (s0, s1), (c0, c1), (h0, h1), (r0, r1), (i0, i1), (a0, a1)

    def stage(t, slot):
        yield from pair_products(t, rows, codes, left, right, weights, 0, 32, 32, 0, squares[slot])
        yield from pair_products(t, rows, codes, left, right, weights, 64, 48, 32, 32, closings[slot])
        for group in GROUPS:
            columns = [hright[source_row(rows, t, k)] for k in group]
            sources = columns[0] if len(columns) == 1 else jnp.concatenate(columns, 1)
            heats[slot][:, LANES * group[0] : LANES * (group[-1] + 1)] = dot(hleft[t], sources, ((0,), (0,)))
            yield
        for f in range(4):
            row = source_row(rows, t, 5 + f)
            shifted[slot][f] = per_source[row] + shift[codes[t * 4 + f]] * per_source[row, 2:3, :]
        for at in range(2):
            own[slot][:, LANES * at : LANES * (at + 1)] = jnp.broadcast_to(per_source[t, at : at + 1, :], (LANES, LANES)).T

    def work(t, slot):
        views = [per_source.at[source_row(rows, t, k)] if k < 5 else shifted[slot].at[k - 5] for k in range(LINKS)]
        for o in range(16):
            eight = slice(8 * o, 8 * o + 8)
            rho_i = own[slot][eight, 0:LANES]
            p_i = own[slot][eight, LANES : 2 * LANES]
            totals = [None] * 5
            for k in range(LINKS):
                lanes = slice(LANES * k, LANES * (k + 1))
                view = views[k]
                s = jnp.maximum(squares[slot][eight, lanes], TINY)
                w = jnp.maximum(1.0 - s * lax.rsqrt(s), 0.0)
                w3 = w * w * w
                z = w3 * pl.reciprocal(s + SOFT, approx=True)
                viscous = jnp.maximum(closings[slot][eight, lanes], 0.0) * pl.reciprocal(rho_i + view[0:1, :], approx=True)
                coupling = (p_i + view[1:2, :]) * w3 + viscous * z
                terms = [coupling * view[2 + at : 3 + at, :] for at in range(4)]
                terms.append((s * z) * heats[slot][eight, lanes])
                totals = [term if total is None else total + term for total, term in zip(totals, terms)]
            for at in range(5):
                sums[slot][eight, LANES * at : LANES * (at + 1)] = totals[at]
            yield

    def close(t, slot):
        got = [jnp.sum(sums[slot][:, LANES * at : LANES * (at + 1)].T, 0, keepdims=True) for at in range(5)]
        living = state[t, 7:8, :] > 0.0
        fluid = 1.0 - state[t, 8:9, :]
        lines = []
        for k in range(3):
            push = SLOPE * (state[t, k : k + 1, :] * got[0] - got[1 + k])
            if k == 2:
                push = push - GRAVITY
            lines.append(jnp.where(living, push * fluid, 0.0))
        out_a[t] = jnp.concatenate(lines, 0)
        out_h[pl.ds(t, 1), :] = jnp.where(living, -SLOPE * got[4] * per_source[t, 6:7, :], 0.0)

    paired_loop(stage, work, close)


SMEM = pl.BlockSpec(memory_space=pltpu.SMEM)
VMEM = pl.BlockSpec(memory_space=pltpu.VMEM)


def density_call(rows, codes, state, place_left, place_right, weights):
    wide = (LANES, LINKS * LANES)
    return pl.pallas_call(
        density_kernel,
        out_shape=jax.ShapeDtypeStruct((SLOTS, LANES), F32),
        in_specs=[SMEM] * 2 + [VMEM] * 4,
        out_specs=VMEM,
        scratch_shapes=[
            pltpu.VMEM((SLOTS, 64, LANES), BF16),
            pltpu.VMEM((SOURCES, 64, LANES), BF16),
            pltpu.VMEM(wide, F32), pltpu.VMEM(wide, F32),
            pltpu.VMEM((LANES, LANES), F32), pltpu.VMEM((LANES, LANES), F32),
        ],
        compiler_params=pltpu.CompilerParams(vmem_limit_bytes=32 << 20),
        name="density_pass",
    )(rows, codes, state, place_left, place_right, weights)


def force_call(rows, codes, state, rho_table, place_left, place_right, heat_left, heat_right, weights, shift):
    wide = (LANES, LINKS * LANES)
    return pl.pallas_call(
        force_kernel,
        out_shape=(
            jax.ShapeDtypeStruct((SLOTS, 3, LANES), F32),
            jax.ShapeDtypeStruct((SLOTS, LANES), F32),
        ),
        in_specs=[SMEM] * 2 + [VMEM] * 8,
        out_specs=(VMEM, VMEM),
        scratch_shapes=[
            pltpu.VMEM((SLOTS, 144, LANES), BF16),
            pltpu.VMEM((SOURCES, 144, LANES), BF16),
            pltpu.VMEM((SLOTS, 32, LANES), BF16),
            pltpu.VMEM((SOURCES, 32, LANES), BF16),
            pltpu.VMEM((SOURCES, 8, LANES), F32),
        ]
        + [pltpu.VMEM(wide, F32)] * 6
        + [pltpu.VMEM((4, 8, LANES), F32)] * 2
        + [pltpu.VMEM((LANES, 2 * LANES), F32)] * 2
        + [pltpu.VMEM((LANES, 5 * LANES), F32)] * 2,
        compiler_params=pltpu.CompilerParams(vmem_limit_bytes=48 << 20),
        name="force_pass",
    )(rows, codes, state, rho_table, place_left, place_right, heat_left, heat_right, weights, shift)


def padded(shard, sides, width):
    for axis, dim in sides:
        size, length = (lax.axis_size(axis), shard.shape[dim])
        up = [(i, (i + 1) % size) for i in range(size - 1)]
        down = [(j, i) for i, j in up]
        last = lax.slice_in_dim(shard, length - width, length, axis=dim)
        first = lax.slice_in_dim(shard, 0, width, axis=dim)
        before = lax.ppermute(last, axis, up)
        after = lax.ppermute(first, axis, down)
        shard = jnp.concatenate([before, shard, after], axis=dim)
    return shard


def eight_around(haloed):
    flat = haloed.reshape((9,) + haloed.shape[2:])
    picked = jnp.concatenate([flat[:4], flat[5:]], 0)
    return picked.reshape((8 * haloed.shape[2],) + haloed.shape[3:])


def owner(x, core, z, y):
    return (2 * (x % 4) + core) * N_GY + 4 * (z % 4) + y % 4


CHIPS = [(x, c, z, y) for x in range(4) for c in range(2) for z in range(4) for y in range(4)]
STAGES = (
    [(0, 0, k, 0) for k in (1, 2, 3)],
    [(0, 0, 0, k) for k in (1, 2, 3)],
    [(k, 0, 0, 0) for k in (1, 2, 3)],
    [(0, 1, 0, 0)],
)


def gather_all(shard):
    for stage in STAGES:
        pieces = [shard]
        for dx, dc, dz, dy in stage:
            pairs = [(owner(x, c, z, y), owner(x + dx, c ^ dc, z + dz, y + dy)) for x, c, z, y in CHIPS]
            pieces.append(lax.ppermute(shard, ("gx", "gy"), pairs))
        shard = jnp.concatenate(pieces, 0)
    return shard


def place_of(gx, gy):
    number = jnp.arange(N_GX * N_GY * MIG)
    ox, oy = number // (MIG * N_GY), number // MIG % N_GY
    core = gx % 2 ^ ox % 2
    x = (gx // 2 - ox // 2) % 4
    z = (gy // 4 - oy // 4) % 4
    y = (gy - oy) % 4
    return (((core * 4 + x) * 4 + y) * 4 + z) * MIG + number % MIG


def local(
    cell_local_coords,
    particle_speeds,
    thermal_state,
    particle_weights,
    boundary_flag,
    departing_local_groups,
    migrant_target_holder,
    target_entry_inputs,
    adjacent_cell_label,
):
    gx, gy = lax.axis_index("gx"), lax.axis_index("gy")
    state_tables = jnp.concatenate(
        [
            cell_local_coords,
            particle_speeds,
            thermal_state[:, None, :],
            particle_weights[:, None, :],
            boundary_flag.astype(jnp.float32)[:, None, :],
        ],
        1,
    )
    width = state_tables.shape[1]
    lanes = state_tables.shape[2]
    chosen = departing_local_groups[0]
    leaving = jnp.take(state_tables, chosen, axis=0)
    numbers = jnp.arange(state_tables.shape[0])
    departed = jnp.any(numbers[:, None] == chosen[None, :], 1)
    staying = jnp.where(departed[:, None, None], 0.0, state_tables)
    edge = BND - IN_CAP
    haloed = padded(staying[:edge].reshape((1, 1, edge * width, lanes)), (("gx", 0), ("gy", 1)), 1)
    around = haloed.reshape((9, edge, width, lanes))
    near_x = gx + jnp.array([-1, -1, -1, 0, 0, 0, 1, 1, 1])
    near_y = gy + jnp.array([-1, 0, 1, -1, 0, 1, -1, 0, 1])
    inside = (near_x >= 0) & (near_x < N_GX) & (near_y >= 0) & (near_y < N_GY)
    match = migrant_target_holder.reshape(-1)[None, :] == (near_x * N_GY + near_y)[:, None]
    match = match & inside[:, None]
    ranking = jnp.cumsum(match.astype(jnp.int32), axis=1) - 1
    taken = match[:, None, :] & (ranking[:, None, :] == jnp.arange(IN_CAP)[None, :, None])
    places = place_of(gx, gy)
    wanted = jnp.sum(jnp.where(taken, places[None, None, :], 0), 2)
    present = jnp.any(taken, 2)
    incoming = gather_all(leaving.reshape(MIG * width, lanes)).reshape(-1, width, lanes)
    arrived = jnp.where(present[:, :, None, None], jnp.take(incoming, wanted, axis=0), 0.0)
    first = jnp.concatenate([arrived, around], 1)
    ghosts = jnp.concatenate([first[:4], first[5:]], 0).reshape((-1, width, lanes))
    state = jnp.concatenate([arrived[4], staying, ghosts], 0)
    rows = target_entry_inputs.reshape(-1)
    codes = (adjacent_cell_label + (adjacent_cell_label >= 13).astype(jnp.int32)).reshape(-1)
    left, right, weights, shift = pair_rows()
    heat_left, heat_right = heat_rows()
    left, right, weights, heat_left, heat_right = (
        jnp.asarray(a, BF16) for a in (left, right, weights, heat_left, heat_right)
    )
    shift = jnp.asarray(shift)
    density = density_call(rows, codes, state, left[:64], right[:64], weights)
    again = eight_around(
        padded(density[:BND].reshape((1, 1, BND, lanes)), (("gx", 0), ("gy", 1)), 1)
    )
    rho_table = jnp.concatenate([density, again], 0)
    acceleration, heating = force_call(
        rows, codes, state, rho_table, left, right, heat_left, heat_right, weights, shift
    )
    return density, acceleration, heating


def solution(mesh):
    return jax.shard_map(
        local,
        mesh=mesh,
        in_specs=(
            P(("gx", "gy"), None, None),
            P(("gx", "gy"), None, None),
            P(("gx", "gy"), None),
            P(("gx", "gy"), None),
            P(("gx", "gy"), None),
            P(("gx", "gy"), None),
            P(),
            P(("gx", "gy"), None),
            P(("gx", "gy"), None),
        ),
        out_specs=(P(("gx", "gy"), None), P(("gx", "gy"), None, None), P(("gx", "gy"), None)),
        check_vma=False,
    )
```

```python
import functools
import math

import jax
import jax.numpy as jnp
import numpy as np
from jax import lax
from jax.experimental import pallas as pl
from jax.experimental.pallas import tpu as pltpu
from jax.sharding import PartitionSpec as P

IN_CAP = 8
BND = 16
MIG = 2
N_GX = 8
N_GY = 16
SLOTS = 104
SOURCES = 232
LANES = 128
LINKS = 9

SMOOTH = 0.5
KERNEL = 21.0 / (16.0 * math.pi * SMOOTH**3)
SOUND = math.sqrt(7.0)
VISC = 0.1
SOFT = 0.01 * SMOOTH**2
GRAVITY = 1.0
KAPPA = -2.0 * VISC * SOUND * SMOOTH
SLOPE = 5.0 * KERNEL / SMOOTH**2
TINY = 1e-30

F32 = jnp.float32
BF16 = jnp.bfloat16

PARTS = ((0, 0), (0, 1), (0, 2), (1, 0), (1, 1), (2, 0))
ONE = 24
STILL = 64
SHIFTED = 112


def part(p, channel):
    return 8 * p + channel


def source_at(p_target, p_source, channel):
    return 48 + channel if p_source == 2 else 16 * p_target + 8 * p_source + channel


def pair_rows():
    square = np.zeros((SHIFTED, 32), np.float32)
    closing = np.zeros((SHIFTED, 32), np.float32)
    steps = np.array([(c // 9 - 1, c // 3 % 3 - 1, c % 3 - 1) for c in range(27)], np.float32)
    weights = np.zeros((32, SHIFTED - STILL), np.float32)
    for k in range(3):
        for a, b in PARTS:
            square[source_at(a, b, k), part(a, k)] = -2
            closing[source_at(a, b, k), part(a, 3 + k)] = -1
            closing[source_at(a, b, 3 + k), part(a, k)] = -1
        for p in range(3):
            row = 64 + 8 * p
            square[row + k, ONE] = 2
            closing[row + 3 + k, ONE] = 1
            weights[:27, 8 * p + k] = weights[:27, 8 * p + 3 + k] = steps[:, k]
            row = (88, 96, 99)[p] + k
            square[row, part(p, k)] = -2
            closing[row, part(p, 3 + k)] = -1
            weights[:27, row - 64] = steps[:, k]
    for p in range(3):
        square[source_at(0, p, 6), ONE] = 1
        square[56 + p, part(p, 6)] = 1
        closing[source_at(0, p, 7), ONE] = 1
        closing[56 + p, part(p, 7)] = 1
    square[91, ONE] = 1
    weights[:27, 91 - 64] = (steps * steps).sum(1)
    shift = np.zeros((32, 8, LANES), np.float32)
    shift[:27, :3] = steps[:, :, None]
    weights = np.broadcast_to(weights[:, :, None], weights.shape + (LANES,))
    return square, closing, weights, shift


def heat_rows():
    heat, rho = (np.zeros((STILL, 32), np.float32) for _ in range(2))
    for a, b in PARTS:
        heat[source_at(a, b, 0), part(a, 0)] = 1
        heat[source_at(a, b, 1), part(a, 1)] = 1
    for p in range(3):
        heat[source_at(0, p, 2), ONE] = -1
        heat[source_at(0, p, 3), part(0, 2)] = -1
        rho[source_at(0, p, 4), ONE] = 1
        rho[56 + p, part(p, 3)] = 1
    return np.concatenate([heat, rho])


def split(block):
    high = block.astype(BF16).astype(F32)
    rest = block - high
    middle = rest.astype(BF16).astype(F32)
    return high, middle, rest - middle


def parts_of(block):
    return jnp.concatenate([*split(block), jnp.ones_like(block)], 0).astype(BF16)


def stacked(parts, row, lanes_weights=None, ones=False):
    first, second = parts[row, 0:16, :], parts[row, 16:32, :]
    rows = [first, first, first, second]
    if ones:
        more = [first, second, jnp.ones_like(first)]
        if lanes_weights is not None:
            more = [lanes_weights[16 * q : 16 * q + 16, :] * tile for q, tile in enumerate(more)]
        rows += more
    return jnp.concatenate(rows, 0)


def channels(state, b):
    x = state[b, 0:3, :]
    v = state[b, 3:6, :] * KAPPA
    n = jnp.sum(x * x, 0, keepdims=True)
    vx = jnp.sum(x * v, 0, keepdims=True)
    return jnp.concatenate([x, v, n, vx], 0)


def dot(a, b, contract):
    return lax.dot_general(a, b, (contract, ((), ())), preferred_element_type=F32)


def build_targets(place, parts, out, rows, first, count):
    for u in range(count // 2):
        at = first + 2 * u
        both = jnp.concatenate([parts[at], parts[at + 1]], 1)
        got = dot(place[...], both, ((1,), (0,))).astype(BF16)
        for q in range(2):
            for g in range(got.shape[0] // rows):
                out[at + q, :, LANES * g : LANES * (g + 1)] = got[rows * g : rows * (g + 1), LANES * q : LANES * (q + 1)]


def build_tables(own, other, targets):
    def first(u, carry):
        targets(8 * jnp.maximum(u - 1, 0), 8)
        for q in range(8):
            own(8 * jnp.minimum(u, SLOTS // 8 - 1) + q)
        return carry

    def second(u, carry):
        for q in range(8):
            other(8 * u + q)
        return carry

    lax.fori_loop(0, SLOTS // 8 + 1, first, 0)
    lax.fori_loop(SLOTS // 8, SOURCES // 8, second, 0)


def source_row(rows, t, k):
    return t if k == 0 else rows[t * 8 + k - 1]


def run(steps):
    for _ in steps:
        pass


def alternate(*steps):
    live = list(steps)
    while live:
        for g in list(live):
            if next(g, live) is live:
                live.remove(g)


def paired_loop(stage, work, close, batch):
    last = SLOTS // batch - 1
    span = lambda n: [n * batch + q for q in range(batch)]

    def chain(piece, n, slot):
        for q, t in enumerate(span(n)):
            yield from piece(t, slot * batch + q)

    run(chain(stage, 0, 0))

    def step(n, carry):
        for slot in range(2):

            @pl.when(lax.rem(n, 2) == slot)
            def _():
                alternate(
                    chain(close, jnp.maximum(n - 1, 0), 1 - slot),
                    chain(work, n, slot),
                    chain(stage, jnp.minimum(n + 1, last), 1 - slot),
                )

        return carry

    lax.fori_loop(0, last + 1, step, 0)
    run(chain(close, last, last % 2))


GROUPS = ((0, 1), (2, 3), (4,), (5, 6), (7, 8))


def density_kernel(rows, codes, state, place, weights, out, parts, left, *buffers):
    squares, sums = buffers[: 2 * DENSITY_BATCH], buffers[2 * DENSITY_BATCH :]

    def each(b):
        parts[b] = parts_of(channels(state, b))

    build_tables(each, each, lambda t, count: build_targets(place, parts, left, SHIFTED, t, count))

    def stage(t, slot):
        near, far = left[t, 0:STILL, :], left[t]
        for group in GROUPS:
            face = group[0] >= 5
            columns = [
                stacked(parts, source_row(rows, t, k), weights[codes[t * 4 + k - 5]] if face else None, face)
                for k in group
            ]
            sources = columns[0] if len(columns) == 1 else jnp.concatenate(columns, 1)
            made = dot(far if face else near, sources, ((0,), (0,)))
            squares[slot][:, LANES * group[0] : LANES * (group[-1] + 1)] = made
            yield

    def work(t, slot):
        square = squares[slot]
        masses = [state.at[source_row(rows, t, k)] for k in range(LINKS)]
        for o in range(16):
            total = None
            for k in range(LINKS):
                s = jnp.maximum(square[8 * o : 8 * o + 8, LANES * k : LANES * (k + 1)], TINY)
                w = jnp.maximum(1.0 - s * lax.rsqrt(s), 0.0)
                w2 = w * w
                term = (w2 * w2) * (1.25 - w) * masses[k][7:8, :]
                total = term if total is None else total + term
            sums[slot][8 * o : 8 * o + 8, :] = total
            if o % 3 == 0:
                yield

    def close(t, slot):
        rho = jnp.sum(sums[slot][...].T, 0, keepdims=True) * (4.0 * KERNEL)
        out[pl.ds(t, 1), :] = jnp.where(state[t, 7:8, :] > 0.0, rho, 0.0)
        yield

    paired_loop(stage, work, close, DENSITY_BATCH)


def force_kernel(rows, codes, state, rho_table, place, heat_place, weights, shift, out_a, out_h,
                 parts, heat_parts, own_parts, mass_parts, pressures, own_pressure, left, heat_left, *buffers):
    pairs, heats, split_terms, heat_sums = (buffers[2 * FORCE_BATCH * q : 2 * FORCE_BATCH * (q + 1)] for q in range(4))

    def each(b):
        parts[b] = parts_of(channels(state, b))
        x, heat, mass, wall = state[b, 0:3, :], state[b, 6:7, :], state[b, 7:8, :], state[b, 8:9, :]
        rho = jnp.where(mass > 0.0, rho_table[pl.ds(b, 1), :], 1.0)
        inverse = 1.0 / rho
        r2 = rho * rho
        pressure = (r2 * r2 * r2 * rho - 1.0) * (inverse * inverse)
        ratio = mass * inverse
        a = ratio * (2.0 + 1.2 * wall)
        b2 = ratio * (1.2 + 3.6 * wall)
        zero = jnp.zeros_like(rho)
        heat_parts[b] = parts_of(jnp.concatenate([a, b2, a * heat, b2 * heat, rho, zero, zero, zero], 0))
        pressures[b] = jnp.broadcast_to(pressure, (LANES, LANES)).T
        high, middle, low = split(jnp.concatenate([mass, mass * x, zero, zero, zero, zero], 0))
        mass_parts[b] = jnp.concatenate([high[0:4], middle[0:4], low], 0).astype(BF16)
        return [heat, heat * wall, wall, rho, zero, zero, zero, zero], pressure

    def own(b):
        lines, pressure = each(b)
        own_parts[b] = parts_of(jnp.concatenate(lines, 0))
        own_pressure[pl.ds(b, 1), :] = pressure

    def targets(t, count):
        build_targets(place, parts, left, SHIFTED, t, count)
        build_targets(heat_place, own_parts, heat_left, STILL, t, count)

    build_tables(own, each, targets)

    def stage(t, slot):
        near, heat_near = left[t, 0:STILL, :], heat_left[t]
        for k in range(LINKS):
            row = source_row(rows, t, k)
            if k < 5:
                targets = near
            else:
                scale = weights[codes[t * 4 + k - 5]]
                targets = jnp.concatenate(
                    [near, left[t, STILL:SHIFTED, :] * jnp.concatenate([scale, scale], 1)], 0
                )
            block = slice(LANES * k, LANES * (k + 1))
            pairs[slot][block, :] = dot(stacked(parts, row, None, k >= 5), targets, ((0,), (0,)))
            heats[slot][block, :] = dot(stacked(heat_parts, row), heat_near, ((0,), (0,)))
            yield

    def work(t, slot):
        pair, heat, terms = pairs[slot], heats[slot], split_terms[slot]
        totals = [None] * 2
        pressure = own_pressure[pl.ds(t, 1), :]
        for k in range(LINKS):
            near = pressures.at[source_row(rows, t, k)]
            for o in range(8):
                found = []
                for q in range(2):
                    eight = slice(LANES * k + 16 * o + 8 * q, LANES * k + 16 * o + 8 * q + 8)
                    s = jnp.maximum(pair[eight, 0:LANES], TINY)
                    w = jnp.maximum(1.0 - s * lax.rsqrt(s), 0.0)
                    w3 = w * w * w
                    z = w3 * pl.reciprocal(s + SOFT, approx=True)
                    closing = jnp.maximum(pair[eight, LANES : 2 * LANES], 0.0)
                    viscous = closing * pl.reciprocal(heat[eight, LANES : 2 * LANES], approx=True)
                    sum_p = pressure + near[16 * o + 8 * q : 16 * o + 8 * q + 8, :]
                    found.append(sum_p * w3 + viscous * z)
                    warm = (s * z) * heat[eight, 0:LANES]
                    totals[q] = warm if totals[q] is None else totals[q] + warm
                term = jnp.concatenate(found, 0)
                high = term.astype(BF16)
                at = 2 * LANES * k + 16 * o
                terms[at : at + 16, :] = high
                terms[at + LANES : at + LANES + 16, :] = (term - high.astype(F32)).astype(BF16)
            yield
        heat_sums[slot][...] = totals[0] + totals[1]

    def close(t, slot):
        total, moved = None, [None] * 3
        for k in range(LINKS):
            mass = mass_parts[source_row(rows, t, k)]
            got = dot(
                jnp.concatenate([mass, mass], 1),
                split_terms[slot][2 * LANES * k : 2 * LANES * (k + 1), :],
                ((1,), (0,)),
            )
            total = got if total is None else total + got
            if k >= 5:
                pull = got[0:1] + got[4:5] + got[8:9]
                code = codes[t * 4 + k - 5]
                for axis in range(3):
                    more = shift[code, axis : axis + 1, :] * pull
                    moved[axis] = more if moved[axis] is None else moved[axis] + more
            yield
        total = total[0:4] + total[4:8] + total[8:12]
        mass, fluid = state[t, 7:8, :], 1.0 - state[t, 8:9, :]
        living = mass > 0.0
        lines = []
        for k in range(3):
            push = SLOPE * (state[t, k : k + 1, :] * total[0:1] - (total[1 + k : 2 + k] + moved[k]))
            if k == 2:
                push = push - GRAVITY
            lines.append(jnp.where(living, push * fluid, 0.0))
        out_a[t] = jnp.concatenate(lines, 0)
        warm = jnp.sum(heat_sums[slot][...], 0, keepdims=True)
        rho = jnp.where(living, rho_table[pl.ds(t, 1), :], 1.0)
        out_h[pl.ds(t, 1), :] = jnp.where(living, -SLOPE * warm / rho, 0.0)

    paired_loop(stage, work, close, FORCE_BATCH)


SMEM = pl.BlockSpec(memory_space=pltpu.SMEM)
VMEM = pl.BlockSpec(memory_space=pltpu.VMEM)


DENSITY_BATCH = 4
FORCE_BATCH = 2


def density_call(rows, codes, state, place, weights):
    wide = (LANES, LINKS * LANES)
    return pl.pallas_call(
        density_kernel,
        out_shape=jax.ShapeDtypeStruct((SLOTS, LANES), F32),
        in_specs=[SMEM] * 2 + [VMEM] * 3,
        out_specs=VMEM,
        scratch_shapes=[
            pltpu.VMEM((SOURCES, 32, LANES), BF16),
            pltpu.VMEM((SLOTS, SHIFTED, LANES), BF16),
        ]
        + [pltpu.VMEM(wide, F32)] * (2 * DENSITY_BATCH)
        + [pltpu.VMEM((LANES, LANES), F32)] * (2 * DENSITY_BATCH),
        compiler_params=pltpu.CompilerParams(vmem_limit_bytes=32 << 20),
        name="density_pass",
    )(rows, codes, state, place, weights)


def force_call(rows, codes, state, rho_table, place, heat_place, weights, shift):
    tall = LINKS * LANES
    return pl.pallas_call(
        force_kernel,
        out_shape=(
            jax.ShapeDtypeStruct((SLOTS, 3, LANES), F32),
            jax.ShapeDtypeStruct((SLOTS, LANES), F32),
        ),
        in_specs=[SMEM] * 2 + [VMEM] * 6,
        out_specs=(VMEM, VMEM),
        scratch_shapes=[
            pltpu.VMEM((SOURCES, 32, LANES), BF16),
            pltpu.VMEM((SOURCES, 32, LANES), BF16),
            pltpu.VMEM((SLOTS, 32, LANES), BF16),
            pltpu.VMEM((SOURCES, 16, LANES), BF16),
            pltpu.VMEM((SOURCES, LANES, LANES), F32),
            pltpu.VMEM((SLOTS, LANES), F32),
            pltpu.VMEM((SLOTS, SHIFTED, 2 * LANES), BF16),
            pltpu.VMEM((SLOTS, STILL, 2 * LANES), BF16),
        ]
        + [pltpu.VMEM((tall, 2 * LANES), F32)] * (2 * FORCE_BATCH)
        + [pltpu.VMEM((tall, 2 * LANES), F32)] * (2 * FORCE_BATCH)
        + [pltpu.VMEM((2 * tall, LANES), BF16)] * (2 * FORCE_BATCH)
        + [pltpu.VMEM((8, LANES), F32)] * (2 * FORCE_BATCH),
        compiler_params=pltpu.CompilerParams(vmem_limit_bytes=48 << 20),
        name="force_pass",
    )(rows, codes, state, rho_table, place, heat_place, weights, shift)


def padded(shard, sides, width):
    for axis, dim in sides:
        size, length = (lax.axis_size(axis), shard.shape[dim])
        up = [(i, (i + 1) % size) for i in range(size - 1)]
        down = [(j, i) for i, j in up]
        last = lax.slice_in_dim(shard, length - width, length, axis=dim)
        first = lax.slice_in_dim(shard, 0, width, axis=dim)
        before = lax.ppermute(last, axis, up)
        after = lax.ppermute(first, axis, down)
        shard = jnp.concatenate([before, shard, after], axis=dim)
    return shard


def eight_around(haloed):
    flat = haloed.reshape((9,) + haloed.shape[2:])
    picked = jnp.concatenate([flat[:4], flat[5:]], 0)
    return picked.reshape((8 * haloed.shape[2],) + haloed.shape[3:])


def owner(x, core, z, y):
    return (2 * (x % 4) + core) * N_GY + 4 * (z % 4) + y % 4


CHIPS = [(x, c, z, y) for x in range(4) for c in range(2) for z in range(4) for y in range(4)]
STAGES = (
    [(0, 0, k, 0) for k in (1, 2, 3)],
    [(0, 0, 0, k) for k in (1, 2, 3)],
    [(k, 0, 0, 0) for k in (1, 2, 3)],
    [(0, 1, 0, 0)],
)


def gather_all(shard):
    for stage in STAGES:
        pieces = [shard]
        for dx, dc, dz, dy in stage:
            pairs = [(owner(x, c, z, y), owner(x + dx, c ^ dc, z + dz, y + dy)) for x, c, z, y in CHIPS]
            pieces.append(lax.ppermute(shard, ("gx", "gy"), pairs))
        shard = jnp.concatenate(pieces, 0)
    return shard


def place_of(gx, gy):
    number = jnp.arange(N_GX * N_GY * MIG)
    ox, oy = number // (MIG * N_GY), number // MIG % N_GY
    core = gx % 2 ^ ox % 2
    x = (gx // 2 - ox // 2) % 4
    z = (gy // 4 - oy // 4) % 4
    y = (gy - oy) % 4
    return (((core * 4 + x) * 4 + y) * 4 + z) * MIG + number % MIG


def local(
    cell_local_coords,
    particle_speeds,
    thermal_state,
    particle_weights,
    boundary_flag,
    departing_local_groups,
    migrant_target_holder,
    target_entry_inputs,
    adjacent_cell_label,
):
    gx, gy = lax.axis_index("gx"), lax.axis_index("gy")
    state_tables = jnp.concatenate(
        [
            cell_local_coords,
            particle_speeds,
            thermal_state[:, None, :],
            particle_weights[:, None, :],
            boundary_flag.astype(jnp.float32)[:, None, :],
        ],
        1,
    )
    width = state_tables.shape[1]
    lanes = state_tables.shape[2]
    chosen = departing_local_groups[0]
    leaving = jnp.take(state_tables, chosen, axis=0)
    numbers = jnp.arange(state_tables.shape[0])
    departed = jnp.any(numbers[:, None] == chosen[None, :], 1)
    staying = jnp.where(departed[:, None, None], 0.0, state_tables)
    edge = BND - IN_CAP
    haloed = padded(staying[:edge].reshape((1, 1, edge * width, lanes)), (("gx", 0), ("gy", 1)), 1)
    around = haloed.reshape((9, edge, width, lanes))
    near_x = gx + jnp.array([-1, -1, -1, 0, 0, 0, 1, 1, 1])
    near_y = gy + jnp.array([-1, 0, 1, -1, 0, 1, -1, 0, 1])
    inside = (near_x >= 0) & (near_x < N_GX) & (near_y >= 0) & (near_y < N_GY)
    match = migrant_target_holder.reshape(-1)[None, :] == (near_x * N_GY + near_y)[:, None]
    match = match & inside[:, None]
    ranking = jnp.cumsum(match.astype(jnp.int32), axis=1) - 1
    taken = match[:, None, :] & (ranking[:, None, :] == jnp.arange(IN_CAP)[None, :, None])
    places = place_of(gx, gy)
    wanted = jnp.sum(jnp.where(taken, places[None, None, :], 0), 2)
    present = jnp.any(taken, 2)
    incoming = gather_all(leaving.reshape(MIG * width, lanes)).reshape(-1, width, lanes)
    arrived = jnp.where(present[:, :, None, None], jnp.take(incoming, wanted, axis=0), 0.0)
    first = jnp.concatenate([arrived, around], 1)
    ghosts = jnp.concatenate([first[:4], first[5:]], 0).reshape((-1, width, lanes))
    state = jnp.concatenate([arrived[4], staying, ghosts], 0)
    rows = target_entry_inputs.reshape(-1)
    codes = (adjacent_cell_label + (adjacent_cell_label >= 13).astype(jnp.int32)).reshape(-1)
    square, closing, weights, shift = pair_rows()
    square, closing, weights, heat_place = (jnp.asarray(a, BF16) for a in (square, closing, weights, heat_rows()))
    place = jnp.concatenate([square, closing], 0)
    density = density_call(rows, codes, state, square, weights)
    again = eight_around(
        padded(density[:BND].reshape((1, 1, BND, lanes)), (("gx", 0), ("gy", 1)), 1)
    )
    rho_table = jnp.concatenate([density, again], 0)
    acceleration, heating = force_call(
        rows, codes, state, rho_table, place, heat_place, weights, jnp.asarray(shift)
    )
    return density, acceleration, heating


def solution(mesh):
    return jax.shard_map(
        local,
        mesh=mesh,
        in_specs=(
            P(("gx", "gy"), None, None),
            P(("gx", "gy"), None, None),
            P(("gx", "gy"), None),
            P(("gx", "gy"), None),
            P(("gx", "gy"), None),
            P(("gx", "gy"), None),
            P(),
            P(("gx", "gy"), None),
            P(("gx", "gy"), None),
        ),
        out_specs=(P(("gx", "gy"), None), P(("gx", "gy"), None, None), P(("gx", "gy"), None)),
        check_vma=False,
    )
```

```python
import functools
import math

import jax
import jax.numpy as jnp
import numpy as np
from jax import lax
from jax.experimental import pallas as pl
from jax.experimental.pallas import tpu as pltpu
from jax.sharding import PartitionSpec as P

IN_CAP = 8
BND = 16
MIG = 2
N_GX = 8
N_GY = 16
SLOTS = 104
SOURCES = 232
LANES = 128
LINKS = 9

SMOOTH = 0.5
KERNEL = 21.0 / (16.0 * math.pi * SMOOTH**3)
SOUND = math.sqrt(7.0)
VISC = 0.1
SOFT = 0.01 * SMOOTH**2
GRAVITY = 1.0
KAPPA = -2.0 * VISC * SOUND * SMOOTH
SLOPE = 5.0 * KERNEL / SMOOTH**2
TINY = 1e-30

F32 = jnp.float32
BF16 = jnp.bfloat16

PARTS = ((0, 0), (0, 1), (0, 2), (1, 0), (1, 1), (2, 0))
ONE = 24
STILL = 64
SHIFTED = 112


def part(p, channel):
    return 8 * p + channel


def source_at(p_target, p_source, channel):
    return 48 + channel if p_source == 2 else 16 * p_target + 8 * p_source + channel


def pair_rows():
    square = np.zeros((SHIFTED, 32), np.float32)
    closing = np.zeros((SHIFTED, 32), np.float32)
    steps = np.array([(c // 9 - 1, c // 3 % 3 - 1, c % 3 - 1) for c in range(27)], np.float32)
    weights = np.zeros((32, SHIFTED - STILL), np.float32)
    for k in range(3):
        for a, b in PARTS:
            square[source_at(a, b, k), part(a, k)] = -2
            closing[source_at(a, b, k), part(a, 3 + k)] = -1
            closing[source_at(a, b, 3 + k), part(a, k)] = -1
        for p in range(3):
            row = 64 + 8 * p
            square[row + k, ONE] = 2
            closing[row + 3 + k, ONE] = 1
            weights[:27, 8 * p + k] = weights[:27, 8 * p + 3 + k] = steps[:, k]
            row = (88, 96, 99)[p] + k
            square[row, part(p, k)] = -2
            closing[row, part(p, 3 + k)] = -1
            weights[:27, row - 64] = steps[:, k]
    for p in range(3):
        square[source_at(0, p, 6), ONE] = 1
        square[56 + p, part(p, 6)] = 1
        closing[source_at(0, p, 7), ONE] = 1
        closing[56 + p, part(p, 7)] = 1
    square[91, ONE] = 1
    weights[:27, 91 - 64] = (steps * steps).sum(1)
    shift = np.zeros((32, 8, LANES), np.float32)
    shift[:27, :3] = steps[:, :, None]
    weights = np.broadcast_to(weights[:, :, None], weights.shape + (LANES,))
    return square, closing, weights, shift


def heat_rows():
    heat, rho = (np.zeros((STILL, 32), np.float32) for _ in range(2))
    for a, b in PARTS:
        heat[source_at(a, b, 0), part(a, 0)] = 1
        heat[source_at(a, b, 1), part(a, 1)] = 1
    for p in range(3):
        heat[source_at(0, p, 2), ONE] = -1
        heat[source_at(0, p, 3), part(0, 2)] = -1
        rho[source_at(0, p, 4), ONE] = 1
        rho[56 + p, part(p, 3)] = 1
    return np.concatenate([heat, rho])


def split(block):
    high = block.astype(BF16).astype(F32)
    rest = block - high
    middle = rest.astype(BF16).astype(F32)
    return high, middle, rest - middle


def parts_of(block):
    return jnp.concatenate([*split(block), jnp.ones_like(block)], 0).astype(BF16)


def stacked(parts, row, lanes_weights=None, ones=False):
    first, second = parts[row, 0:16, :], parts[row, 16:32, :]
    rows = [first, first, first, second]
    if ones:
        more = [first, second, jnp.ones_like(first)]
        if lanes_weights is not None:
            more = [lanes_weights[16 * q : 16 * q + 16, :] * tile for q, tile in enumerate(more)]
        rows += more
    return jnp.concatenate(rows, 0)


def channels(state, b):
    x = state[b, 0:3, :]
    v = state[b, 3:6, :] * KAPPA
    n = jnp.sum(x * x, 0, keepdims=True)
    vx = jnp.sum(x * v, 0, keepdims=True)
    return jnp.concatenate([x, v, n, vx], 0)


def dot(a, b, contract):
    return lax.dot_general(a, b, (contract, ((), ())), preferred_element_type=F32)


def build_targets(place, parts, out, rows, first, count):
    for u in range(count // 2):
        at = first + 2 * u
        both = jnp.concatenate([parts[at], parts[at + 1]], 1)
        got = dot(place[...], both, ((1,), (0,))).astype(BF16)
        for q in range(2):
            for g in range(got.shape[0] // rows):
                out[at + q, :, LANES * g : LANES * (g + 1)] = got[rows * g : rows * (g + 1), LANES * q : LANES * (q + 1)]


def build_tables(own, other, targets):
    def first(u, carry):
        for q in range(26):
            own(26 * u + q)
        targets(26 * u, 26)
        return carry

    def second(u, carry):
        for q in range(32):
            other(SLOTS + 32 * u + q)
        return carry

    lax.fori_loop(0, SLOTS // 26, first, 0)
    lax.fori_loop(0, (SOURCES - SLOTS) // 32, second, 0)


def source_row(rows, t, k):
    return t if k == 0 else rows[t * 8 + k - 1]


def run(steps):
    for _ in steps:
        pass


def alternate(*steps):
    live = list(steps)
    while live:
        for g in list(live):
            if next(g, live) is live:
                live.remove(g)


def paired_loop(stage, work, close, batch):
    last = SLOTS // batch - 1
    span = lambda n: [n * batch + q for q in range(batch)]

    def chain(piece, n, slot):
        for q, t in enumerate(span(n)):
            yield from piece(t, slot * batch + q)

    run(chain(stage, 0, 0))

    def step(n, carry):
        for slot in range(2):

            @pl.when(lax.rem(n, 2) == slot)
            def _():
                alternate(
                    chain(close, jnp.maximum(n - 1, 0), 1 - slot),
                    chain(work, n, slot),
                    chain(stage, jnp.minimum(n + 1, last), 1 - slot),
                )

        return carry

    lax.fori_loop(0, last + 1, step, 0)
    run(chain(close, last, last % 2))


GROUPS = ((0, 1), (2, 3), (4,), (5, 6), (7, 8))


def density_kernel(rows, codes, state, place, weights, out, parts, left, *buffers):
    squares, sums = buffers[: 2 * DENSITY_BATCH], buffers[2 * DENSITY_BATCH :]

    def each(b):
        parts[b] = parts_of(channels(state, b))

    build_tables(each, each, lambda t, count: build_targets(place, parts, left, SHIFTED, t, count))

    def stage(t, slot):
        near, far = left[t, 0:STILL, :], left[t]
        for group in GROUPS:
            face = group[0] >= 5
            columns = [
                stacked(parts, source_row(rows, t, k), weights[codes[t * 4 + k - 5]] if face else None, face)
                for k in group
            ]
            sources = columns[0] if len(columns) == 1 else jnp.concatenate(columns, 1)
            made = dot(far if face else near, sources, ((0,), (0,)))
            squares[slot][:, LANES * group[0] : LANES * (group[-1] + 1)] = made
            yield

    def work(t, slot):
        square = squares[slot]
        masses = [state.at[source_row(rows, t, k)] for k in range(LINKS)]
        for o in range(16):
            total = None
            for k in range(LINKS):
                s = jnp.maximum(square[8 * o : 8 * o + 8, LANES * k : LANES * (k + 1)], TINY)
                w = jnp.maximum(1.0 - s * lax.rsqrt(s), 0.0)
                w2 = w * w
                term = (w2 * w2) * (1.25 - w) * masses[k][7:8, :]
                total = term if total is None else total + term
            sums[slot][8 * o : 8 * o + 8, :] = total
            if o % 3 == 0:
                yield

    def close(t, slot):
        rho = jnp.sum(sums[slot][...].T, 0, keepdims=True) * (4.0 * KERNEL)
        out[pl.ds(t, 1), :] = jnp.where(state[t, 7:8, :] > 0.0, rho, 0.0)
        yield

    paired_loop(stage, work, close, DENSITY_BATCH)


def force_kernel(rows, codes, state, rho_table, place, heat_place, weights, shift, out_a, out_h,
                 parts, heat_parts, own_parts, mass_parts, pressures, own_pressure, left, heat_left, *buffers):
    pairs, heats, split_terms, heat_sums = (buffers[2 * FORCE_BATCH * q : 2 * FORCE_BATCH * (q + 1)] for q in range(4))

    row = lax.broadcasted_iota(jnp.int32, (32, LANES), 0)
    pick = jnp.where((row % 8 == 5) & (row < 24), 1.0, 0.0).astype(BF16)

    def each(b, b_own=False):
        parts[b] = parts_of(channels(state, b))
        x, heat, mass, wall = state[b, 0:3, :], state[b, 6:7, :], state[b, 7:8, :], state[b, 8:9, :]
        rho = jnp.where(mass > 0.0, rho_table[pl.ds(b, 1), :], 1.0)
        inverse = 1.0 / rho
        r2 = rho * rho
        pressure = (r2 * r2 * r2 * rho - 1.0) * (inverse * inverse)
        ratio = mass * inverse
        a = ratio * (2.0 + 1.2 * wall)
        b2 = ratio * (1.2 + 3.6 * wall)
        zero = jnp.zeros_like(rho)
        heat_parts[b] = parts_of(jnp.concatenate([a, b2, a * heat, b2 * heat, rho, pressure, zero, zero], 0))
        if b_own:
            pressures[b] = jnp.broadcast_to(pressure, (LANES, LANES)).T
        else:
            pressures[b] = dot(heat_parts[b], pick, ((0,), (0,)))
        high, middle, low = split(jnp.concatenate([mass, mass * x, zero, zero, zero, zero], 0))
        mass_parts[b] = jnp.concatenate([high[0:4], middle[0:4], low], 0).astype(BF16)
        return [heat, heat * wall, wall, rho, zero, zero, zero, zero], pressure

    def own(b):
        lines, pressure = each(b, True)
        own_parts[b] = parts_of(jnp.concatenate(lines, 0))
        own_pressure[pl.ds(b, 1), :] = pressure

    def targets(t, count):
        build_targets(place, parts, left, SHIFTED, t, count)
        build_targets(heat_place, own_parts, heat_left, STILL, t, count)

    build_tables(own, each, targets)

    def stage(t, slot):
        near, heat_near = left[t, 0:STILL, :], heat_left[t]
        for k in range(LINKS):
            row = source_row(rows, t, k)
            if k < 5:
                targets = near
            else:
                scale = weights[codes[t * 4 + k - 5]]
                targets = jnp.concatenate(
                    [near, left[t, STILL:SHIFTED, :] * jnp.concatenate([scale, scale], 1)], 0
                )
            block = slice(LANES * k, LANES * (k + 1))
            pairs[slot][block, :] = dot(stacked(parts, row, None, k >= 5), targets, ((0,), (0,)))
            heats[slot][block, :] = dot(stacked(heat_parts, row), heat_near, ((0,), (0,)))
            yield

    def work(t, slot):
        pair, heat, terms = pairs[slot], heats[slot], split_terms[slot]
        totals = [None] * 2
        pressure = own_pressure[pl.ds(t, 1), :]
        for k in range(LINKS):
            near = pressures.at[source_row(rows, t, k)]
            for o in range(8):
                found = []
                for q in range(2):
                    eight = slice(LANES * k + 16 * o + 8 * q, LANES * k + 16 * o + 8 * q + 8)
                    s = jnp.maximum(pair[eight, 0:LANES], TINY)
                    w = jnp.maximum(1.0 - s * lax.rsqrt(s), 0.0)
                    w3 = w * w * w
                    z = w3 * pl.reciprocal(s + SOFT, approx=True)
                    closing = jnp.maximum(pair[eight, LANES : 2 * LANES], 0.0)
                    viscous = closing * pl.reciprocal(heat[eight, LANES : 2 * LANES], approx=True)
                    sum_p = pressure + near[16 * o + 8 * q : 16 * o + 8 * q + 8, :]
                    found.append(sum_p * w3 + viscous * z)
                    warm = (s * z) * heat[eight, 0:LANES]
                    totals[q] = warm if totals[q] is None else totals[q] + warm
                term = jnp.concatenate(found, 0)
                high = term.astype(BF16)
                at = 2 * LANES * k + 16 * o
                terms[at : at + 16, :] = high
                terms[at + LANES : at + LANES + 16, :] = (term - high.astype(F32)).astype(BF16)
            yield
        heat_sums[slot][...] = totals[0] + totals[1]

    def close(t, slot):
        total, moved = None, [None] * 3
        for k in range(LINKS):
            mass = mass_parts[source_row(rows, t, k)]
            got = dot(
                jnp.concatenate([mass, mass], 1),
                split_terms[slot][2 * LANES * k : 2 * LANES * (k + 1), :],
                ((1,), (0,)),
            )
            total = got if total is None else total + got
            if k >= 5:
                pull = got[0:1] + got[4:5] + got[8:9]
                code = codes[t * 4 + k - 5]
                for axis in range(3):
                    more = shift[code, axis : axis + 1, :] * pull
                    moved[axis] = more if moved[axis] is None else moved[axis] + more
            yield
        total = total[0:4] + total[4:8] + total[8:12]
        mass, fluid = state[t, 7:8, :], 1.0 - state[t, 8:9, :]
        living = mass > 0.0
        lines = []
        for k in range(3):
            push = SLOPE * (state[t, k : k + 1, :] * total[0:1] - (total[1 + k : 2 + k] + moved[k]))
            if k == 2:
                push = push - GRAVITY
            lines.append(jnp.where(living, push * fluid, 0.0))
        out_a[t] = jnp.concatenate(lines, 0)
        warm = jnp.sum(heat_sums[slot][...], 0, keepdims=True)
        rho = jnp.where(living, rho_table[pl.ds(t, 1), :], 1.0)
        out_h[pl.ds(t, 1), :] = jnp.where(living, -SLOPE * warm / rho, 0.0)

    paired_loop(stage, work, close, FORCE_BATCH)


SMEM = pl.BlockSpec(memory_space=pltpu.SMEM)
VMEM = pl.BlockSpec(memory_space=pltpu.VMEM)


DENSITY_BATCH = 4
FORCE_BATCH = 2


def density_call(rows, codes, state, place, weights):
    wide = (LANES, LINKS * LANES)
    return pl.pallas_call(
        density_kernel,
        out_shape=jax.ShapeDtypeStruct((SLOTS, LANES), F32),
        in_specs=[SMEM] * 2 + [VMEM] * 3,
        out_specs=VMEM,
        scratch_shapes=[
            pltpu.VMEM((SOURCES, 32, LANES), BF16),
            pltpu.VMEM((SLOTS, SHIFTED, LANES), BF16),
        ]
        + [pltpu.VMEM(wide, F32)] * (2 * DENSITY_BATCH)
        + [pltpu.VMEM((LANES, LANES), F32)] * (2 * DENSITY_BATCH),
        compiler_params=pltpu.CompilerParams(vmem_limit_bytes=32 << 20),
        name="density_pass",
    )(rows, codes, state, place, weights)


def force_call(rows, codes, state, rho_table, place, heat_place, weights, shift):
    tall = LINKS * LANES
    return pl.pallas_call(
        force_kernel,
        out_shape=(
            jax.ShapeDtypeStruct((SLOTS, 3, LANES), F32),
            jax.ShapeDtypeStruct((SLOTS, LANES), F32),
        ),
        in_specs=[SMEM] * 2 + [VMEM] * 6,
        out_specs=(VMEM, VMEM),
        scratch_shapes=[
            pltpu.VMEM((SOURCES, 32, LANES), BF16),
            pltpu.VMEM((SOURCES, 32, LANES), BF16),
            pltpu.VMEM((SLOTS, 32, LANES), BF16),
            pltpu.VMEM((SOURCES, 16, LANES), BF16),
            pltpu.VMEM((SOURCES, LANES, LANES), F32),
            pltpu.VMEM((SLOTS, LANES), F32),
            pltpu.VMEM((SLOTS, SHIFTED, 2 * LANES), BF16),
            pltpu.VMEM((SLOTS, STILL, 2 * LANES), BF16),
        ]
        + [pltpu.VMEM((tall, 2 * LANES), F32)] * (2 * FORCE_BATCH)
        + [pltpu.VMEM((tall, 2 * LANES), F32)] * (2 * FORCE_BATCH)
        + [pltpu.VMEM((2 * tall, LANES), BF16)] * (2 * FORCE_BATCH)
        + [pltpu.VMEM((8, LANES), F32)] * (2 * FORCE_BATCH),
        compiler_params=pltpu.CompilerParams(vmem_limit_bytes=48 << 20),
        name="force_pass",
    )(rows, codes, state, rho_table, place, heat_place, weights, shift)


def padded(shard, axis, dim):
    size, here = lax.axis_size(axis), lax.axis_index(axis)
    even = lax.ppermute(shard, axis, [(i, i ^ 1) for i in range(size)])
    odd = lax.ppermute(shard, axis, [(i, (((i - 1) ^ 1) + 1) % size if i else size - 1) for i in range(size)])
    odd = jnp.where((here == 0) | (here == size - 1), 0.0, odd)
    lower = here % 2 == 0
    before, after = jnp.where(lower, odd, even), jnp.where(lower, even, odd)
    return jnp.concatenate([before, shard, after], axis=dim)


def halo(shard):
    return padded(padded(shard[None, None], "gx", 0), "gy", 1)


def eight_around(haloed):
    flat = haloed.reshape((9,) + haloed.shape[2:])
    picked = jnp.concatenate([flat[:4], flat[5:]], 0)
    return picked.reshape((8 * haloed.shape[2],) + haloed.shape[3:])


def owner(x, core, z, y):
    return (2 * x + core) * N_GY + 4 * z + y


CHIPS = [(x, c, z, y) for x in range(4) for c in range(2) for z in range(4) for y in range(4)]
STAGES = (
    [(0, 0, k, 0) for k in (1, 2, 3)],
    [(0, 0, 0, k) for k in (1, 2, 3)],
    [(k, 0, 0, 0) for k in (1, 2, 3)],
    [(0, 1, 0, 0)],
)


def gather_all(shard):
    for stage in STAGES:
        pieces = [shard]
        for dx, dc, dz, dy in stage:
            pairs = [(owner(x, c, z, y), owner(x ^ dx, c ^ dc, z ^ dz, y ^ dy)) for x, c, z, y in CHIPS]
            pieces.append(lax.ppermute(shard, ("gx", "gy"), pairs))
        shard = jnp.concatenate(pieces, 0)
    return shard


def place_of(gx, gy):
    number = jnp.arange(N_GX * N_GY * MIG)
    ox, oy = number // (MIG * N_GY), number // MIG % N_GY
    core = gx % 2 ^ ox % 2
    x = gx // 2 ^ ox // 2
    z = gy // 4 ^ oy // 4
    y = gy % 4 ^ oy % 4
    return (((core * 4 + x) * 4 + y) * 4 + z) * MIG + number % MIG


def local(
    cell_local_coords,
    particle_speeds,
    thermal_state,
    particle_weights,
    boundary_flag,
    departing_local_groups,
    migrant_target_holder,
    target_entry_inputs,
    adjacent_cell_label,
):
    gx, gy = lax.axis_index("gx"), lax.axis_index("gy")
    state_tables = jnp.concatenate(
        [
            cell_local_coords,
            particle_speeds,
            thermal_state[:, None, :],
            particle_weights[:, None, :],
            boundary_flag.astype(jnp.float32)[:, None, :],
        ],
        1,
    )
    width = state_tables.shape[1]
    lanes = state_tables.shape[2]
    chosen = departing_local_groups[0]
    leaving = []
    for k in range(MIG):
        for array in (cell_local_coords, particle_speeds, thermal_state, particle_weights, boundary_flag):
            one = lax.dynamic_index_in_dim(array, chosen[k], 0, False)
            leaving.append(one.reshape(-1, lanes).astype(jnp.float32))
    leaving = jnp.concatenate(leaving, 0)
    numbers = jnp.arange(state_tables.shape[0])
    departed = jnp.any(numbers[:, None] == chosen[None, :], 1)
    staying = jnp.where(departed[:, None, None], 0.0, state_tables)
    edge = BND - IN_CAP
    haloed = halo(staying[:edge].reshape((edge * width, lanes)))
    around = haloed.reshape((9, edge, width, lanes))
    near_x = gx + jnp.array([-1, -1, -1, 0, 0, 0, 1, 1, 1])
    near_y = gy + jnp.array([-1, 0, 1, -1, 0, 1, -1, 0, 1])
    inside = (near_x >= 0) & (near_x < N_GX) & (near_y >= 0) & (near_y < N_GY)
    match = migrant_target_holder.reshape(-1)[None, :] == (near_x * N_GY + near_y)[:, None]
    match = match & inside[:, None]
    ranking = jnp.cumsum(match.astype(jnp.int32), axis=1) - 1
    taken = match[:, None, :] & (ranking[:, None, :] == jnp.arange(IN_CAP)[None, :, None])
    places = place_of(gx, gy)
    wanted = jnp.sum(jnp.where(taken, places[None, None, :], 0), 2)
    present = jnp.any(taken, 2)
    incoming = gather_all(leaving).reshape(-1, width, lanes)
    arrived = jnp.where(present[:, :, None, None], jnp.take(incoming, wanted, axis=0), 0.0)
    first = jnp.concatenate([arrived, around], 1)
    ghosts = jnp.concatenate([first[:4], first[5:]], 0).reshape((-1, width, lanes))
    state = jnp.concatenate([arrived[4], staying, ghosts], 0)
    rows = target_entry_inputs.reshape(-1)
    codes = (adjacent_cell_label + (adjacent_cell_label >= 13).astype(jnp.int32)).reshape(-1)
    square, closing, weights, shift = pair_rows()
    square, closing, weights, heat_place = (jnp.asarray(a, BF16) for a in (square, closing, weights, heat_rows()))
    place = jnp.concatenate([square, closing], 0)
    density = density_call(rows, codes, state, square, weights)
    again = eight_around(halo(density[:BND]))
    rho_table = jnp.concatenate([density, again], 0)
    acceleration, heating = force_call(
        rows, codes, state, rho_table, place, heat_place, weights, jnp.asarray(shift)
    )
    return density, acceleration, heating


def solution(mesh):
    return jax.shard_map(
        local,
        mesh=mesh,
        in_specs=(
            P(("gx", "gy"), None, None),
            P(("gx", "gy"), None, None),
            P(("gx", "gy"), None),
            P(("gx", "gy"), None),
            P(("gx", "gy"), None),
            P(("gx", "gy"), None),
            P(),
            P(("gx", "gy"), None),
            P(("gx", "gy"), None),
        ),
        out_specs=(P(("gx", "gy"), None), P(("gx", "gy"), None, None), P(("gx", "gy"), None)),
        check_vma=False,
    )
```

```python
import functools
import math

import jax
import jax.numpy as jnp
import numpy as np
from jax import lax
from jax.experimental import pallas as pl
from jax.experimental.pallas import tpu as pltpu
from jax.sharding import PartitionSpec as P

IN_CAP = 8
BND = 16
MIG = 2
N_GX = 8
N_GY = 16
SLOTS = 104
SOURCES = 232
LANES = 128
LINKS = 9

SMOOTH = 0.5
KERNEL = 21.0 / (16.0 * math.pi * SMOOTH**3)
SOUND = math.sqrt(7.0)
VISC = 0.1
SOFT = 0.01 * SMOOTH**2
GRAVITY = 1.0
KAPPA = -2.0 * VISC * SOUND * SMOOTH
SLOPE = 5.0 * KERNEL / SMOOTH**2
TINY = 1e-30

F32 = jnp.float32
BF16 = jnp.bfloat16

PARTS = ((0, 0), (0, 1), (0, 2), (1, 0), (1, 1), (2, 0))
ONE = 24
STILL = 64
SHIFTED = 112


def part(p, channel):
    return 8 * p + channel


def source_at(p_target, p_source, channel):
    return 48 + channel if p_source == 2 else 16 * p_target + 8 * p_source + channel


def pair_rows():
    square = np.zeros((SHIFTED, 32), np.float32)
    closing = np.zeros((SHIFTED, 32), np.float32)
    steps = np.array([(c // 9 - 1, c // 3 % 3 - 1, c % 3 - 1) for c in range(27)], np.float32)
    weights = np.zeros((32, SHIFTED - STILL), np.float32)
    for k in range(3):
        for a, b in PARTS:
            square[source_at(a, b, k), part(a, k)] = -2
            closing[source_at(a, b, k), part(a, 3 + k)] = -1
            closing[source_at(a, b, 3 + k), part(a, k)] = -1
        for p in range(3):
            row = 64 + 8 * p
            square[row + k, ONE] = 2
            closing[row + 3 + k, ONE] = 1
            weights[:27, 8 * p + k] = weights[:27, 8 * p + 3 + k] = steps[:, k]
            row = (88, 96, 99)[p] + k
            square[row, part(p, k)] = -2
            closing[row, part(p, 3 + k)] = -1
            weights[:27, row - 64] = steps[:, k]
    for p in range(3):
        square[source_at(0, p, 6), ONE] = 1
        square[56 + p, part(p, 6)] = 1
        closing[source_at(0, p, 7), ONE] = 1
        closing[56 + p, part(p, 7)] = 1
    square[91, ONE] = 1
    weights[:27, 91 - 64] = (steps * steps).sum(1)
    shift = np.zeros((32, 8, LANES), np.float32)
    shift[:27, :3] = steps[:, :, None]
    weights = np.broadcast_to(weights[:, :, None], weights.shape + (LANES,))
    return square, closing, weights, shift


def heat_rows():
    heat, rho = (np.zeros((STILL, 32), np.float32) for _ in range(2))
    for a, b in PARTS:
        heat[source_at(a, b, 0), part(a, 0)] = 1
        heat[source_at(a, b, 1), part(a, 1)] = 1
    for p in range(3):
        heat[source_at(0, p, 2), ONE] = -1
        heat[source_at(0, p, 3), part(0, 2)] = -1
        rho[source_at(0, p, 4), ONE] = 1
        rho[56 + p, part(p, 3)] = 1
    return np.concatenate([heat, rho])


def split(block):
    high = block.astype(BF16).astype(F32)
    rest = block - high
    middle = rest.astype(BF16).astype(F32)
    return high, middle, rest - middle


def parts_of(block):
    return jnp.concatenate([*split(block), jnp.ones_like(block)], 0).astype(BF16)


def stacked(parts, row, lanes_weights=None, ones=False):
    first, second = parts[row, 0:16, :], parts[row, 16:32, :]
    rows = [first, first, first, second]
    if ones:
        more = [first, second, jnp.ones_like(first)]
        if lanes_weights is not None:
            more = [lanes_weights[16 * q : 16 * q + 16, :] * tile for q, tile in enumerate(more)]
        rows += more
    return jnp.concatenate(rows, 0)


def line(state, channel, b):
    return state[channel, pl.ds(b, 1), :]


def channels(state, b):
    x = [line(state, k, b) for k in range(3)]
    v = [line(state, 3 + k, b) * KAPPA for k in range(3)]
    n = x[0] * x[0] + x[1] * x[1] + x[2] * x[2]
    vx = x[0] * v[0] + x[1] * v[1] + x[2] * v[2]
    return jnp.concatenate([*x, *v, n, vx], 0)


def dot(a, b, contract):
    return lax.dot_general(a, b, (contract, ((), ())), preferred_element_type=F32)


def build_targets(place, parts, out, rows, first, count):
    for u in range(count // 2):
        at = first + 2 * u
        both = jnp.concatenate([parts[at], parts[at + 1]], 1)
        got = dot(place[...], both, ((1,), (0,))).astype(BF16)
        for q in range(2):
            for g in range(got.shape[0] // rows):
                out[at + q, :, LANES * g : LANES * (g + 1)] = got[rows * g : rows * (g + 1), LANES * q : LANES * (q + 1)]


def build_tables(own, other, targets):
    def first(u, carry):
        for q in range(26):
            own(26 * u + q)
        targets(26 * u, 26)
        return carry

    def second(u, carry):
        for q in range(32):
            other(SLOTS + 32 * u + q)
        return carry

    lax.fori_loop(0, SLOTS // 26, first, 0)
    lax.fori_loop(0, (SOURCES - SLOTS) // 32, second, 0)


def source_row(rows, t, k):
    return t if k == 0 else rows[t * 8 + k - 1]


def run(steps):
    for _ in steps:
        pass


def alternate(*steps):
    live = list(steps)
    while live:
        for g in list(live):
            if next(g, live) is live:
                live.remove(g)


def paired_loop(stage, work, close, batch):
    last = SLOTS // batch - 1
    span = lambda n: [n * batch + q for q in range(batch)]

    def chain(piece, n, slot):
        for q, t in enumerate(span(n)):
            yield from piece(t, slot * batch + q)

    run(chain(stage, 0, 0))

    def step(n, carry):
        for slot in range(2):

            @pl.when(lax.rem(n, 2) == slot)
            def _():
                alternate(
                    chain(close, jnp.maximum(n - 1, 0), 1 - slot),
                    chain(work, n, slot),
                    chain(stage, jnp.minimum(n + 1, last), 1 - slot),
                )

        return carry

    lax.fori_loop(0, last + 1, step, 0)
    run(chain(close, last, last % 2))


GROUPS = ((0, 1), (2, 3), (4,), (5, 6), (7, 8))


def density_kernel(rows, codes, state, place, weights, out, parts, left, *buffers):
    squares, sums = buffers[: 2 * DENSITY_BATCH], buffers[2 * DENSITY_BATCH :]

    def each(b):
        parts[b] = parts_of(channels(state, b))

    build_tables(each, each, lambda t, count: build_targets(place, parts, left, SHIFTED, t, count))

    def stage(t, slot):
        near, far = left[t, 0:STILL, :], left[t]
        for group in GROUPS:
            face = group[0] >= 5
            columns = [
                stacked(parts, source_row(rows, t, k), weights[codes[t * 4 + k - 5]] if face else None, face)
                for k in group
            ]
            sources = columns[0] if len(columns) == 1 else jnp.concatenate(columns, 1)
            made = dot(far if face else near, sources, ((0,), (0,)))
            squares[slot][:, LANES * group[0] : LANES * (group[-1] + 1)] = made
            yield

    def work(t, slot):
        square = squares[slot]
        row = [source_row(rows, t, k) for k in range(LINKS)]
        for o in range(16):
            total = None
            for k in range(LINKS):
                s = jnp.maximum(square[8 * o : 8 * o + 8, LANES * k : LANES * (k + 1)], TINY)
                w = jnp.maximum(1.0 - s * lax.rsqrt(s), 0.0)
                w2 = w * w
                term = (w2 * w2) * (1.25 - w) * line(state, 7, row[k])
                total = term if total is None else total + term
            sums[slot][8 * o : 8 * o + 8, :] = total
            if o % 3 == 0:
                yield

    def close(t, slot):
        rho = jnp.sum(sums[slot][...].T, 0, keepdims=True) * (4.0 * KERNEL)
        out[pl.ds(t, 1), :] = jnp.where(line(state, 7, t) > 0.0, rho, 0.0)
        yield

    paired_loop(stage, work, close, DENSITY_BATCH)


def force_kernel(rows, codes, state, rho_table, place, heat_place, weights, shift, out_a, out_h,
                 parts, heat_parts, own_parts, mass_parts, pressures, own_pressure, left, heat_left, *buffers):
    pairs, heats, split_terms, heat_sums = (buffers[2 * FORCE_BATCH * q : 2 * FORCE_BATCH * (q + 1)] for q in range(4))

    row = lax.broadcasted_iota(jnp.int32, (32, LANES), 0)
    pick = jnp.where((row % 8 == 5) & (row < 24), 1.0, 0.0).astype(BF16)

    def each(b, b_own=False):
        parts[b] = parts_of(channels(state, b))
        heat, mass, wall = (line(state, channel, b) for channel in (6, 7, 8))
        rho = jnp.where(mass > 0.0, rho_table[pl.ds(b, 1), :], 1.0)
        inverse = 1.0 / rho
        r2 = rho * rho
        pressure = (r2 * r2 * r2 * rho - 1.0) * (inverse * inverse)
        ratio = mass * inverse
        a = ratio * (2.0 + 1.2 * wall)
        b2 = ratio * (1.2 + 3.6 * wall)
        zero = jnp.zeros_like(rho)
        heat_parts[b] = parts_of(jnp.concatenate([a, b2, a * heat, b2 * heat, rho, pressure, zero, zero], 0))
        if b_own:
            pressures[b] = jnp.broadcast_to(pressure, (LANES, LANES)).T
        else:
            pressures[b] = dot(heat_parts[b], pick, ((0,), (0,)))
        high, middle, low = split(
            jnp.concatenate([mass, *(mass * line(state, k, b) for k in range(3)), zero, zero, zero, zero], 0)
        )
        mass_parts[b] = jnp.concatenate([high[0:4], middle[0:4], low], 0).astype(BF16)
        return [heat, heat * wall, wall, rho, zero, zero, zero, zero], pressure

    def own(b):
        lines, pressure = each(b, True)
        own_parts[b] = parts_of(jnp.concatenate(lines, 0))
        own_pressure[pl.ds(b, 1), :] = pressure

    def targets(t, count):
        build_targets(place, parts, left, SHIFTED, t, count)
        build_targets(heat_place, own_parts, heat_left, STILL, t, count)

    build_tables(own, each, targets)

    def stage(t, slot):
        near, heat_near = left[t, 0:STILL, :], heat_left[t]
        for k in range(LINKS):
            row = source_row(rows, t, k)
            if k < 5:
                targets = near
            else:
                scale = weights[codes[t * 4 + k - 5]]
                targets = jnp.concatenate(
                    [near, left[t, STILL:SHIFTED, :] * jnp.concatenate([scale, scale], 1)], 0
                )
            block = slice(LANES * k, LANES * (k + 1))
            pairs[slot][block, :] = dot(stacked(parts, row, None, k >= 5), targets, ((0,), (0,)))
            heats[slot][block, :] = dot(stacked(heat_parts, row), heat_near, ((0,), (0,)))
            yield

    def work(t, slot):
        pair, heat, terms = pairs[slot], heats[slot], split_terms[slot]
        totals = [None] * 2
        pressure = own_pressure[pl.ds(t, 1), :]
        for k in range(LINKS):
            near = pressures.at[source_row(rows, t, k)]
            for o in range(8):
                found = []
                for q in range(2):
                    eight = slice(LANES * k + 16 * o + 8 * q, LANES * k + 16 * o + 8 * q + 8)
                    s = jnp.maximum(pair[eight, 0:LANES], TINY)
                    w = jnp.maximum(1.0 - s * lax.rsqrt(s), 0.0)
                    w3 = w * w * w
                    z = w3 * pl.reciprocal(s + SOFT, approx=True)
                    closing = jnp.maximum(pair[eight, LANES : 2 * LANES], 0.0)
                    viscous = closing * pl.reciprocal(heat[eight, LANES : 2 * LANES], approx=True)
                    sum_p = pressure + near[16 * o + 8 * q : 16 * o + 8 * q + 8, :]
                    found.append(sum_p * w3 + viscous * z)
                    warm = (s * z) * heat[eight, 0:LANES]
                    totals[q] = warm if totals[q] is None else totals[q] + warm
                term = jnp.concatenate(found, 0)
                high = term.astype(BF16)
                at = 2 * LANES * k + 16 * o
                terms[at : at + 16, :] = high
                terms[at + LANES : at + LANES + 16, :] = (term - high.astype(F32)).astype(BF16)
            yield
        heat_sums[slot][...] = totals[0] + totals[1]

    def close(t, slot):
        total, moved = None, [None] * 3
        for k in range(LINKS):
            mass = mass_parts[source_row(rows, t, k)]
            got = dot(
                jnp.concatenate([mass, mass], 1),
                split_terms[slot][2 * LANES * k : 2 * LANES * (k + 1), :],
                ((1,), (0,)),
            )
            total = got if total is None else total + got
            if k >= 5:
                pull = got[0:1] + got[4:5] + got[8:9]
                code = codes[t * 4 + k - 5]
                for axis in range(3):
                    more = shift[code, axis : axis + 1, :] * pull
                    moved[axis] = more if moved[axis] is None else moved[axis] + more
            yield
        total = total[0:4] + total[4:8] + total[8:12]
        mass, fluid = line(state, 7, t), 1.0 - line(state, 8, t)
        living = mass > 0.0
        for k in range(3):
            push = SLOPE * (line(state, k, t) * total[0:1] - (total[1 + k : 2 + k] + moved[k]))
            if k == 2:
                push = push - GRAVITY
            out_a[k, pl.ds(t, 1), :] = jnp.where(living, push * fluid, 0.0)
        warm = jnp.sum(heat_sums[slot][...], 0, keepdims=True)
        rho = jnp.where(living, rho_table[pl.ds(t, 1), :], 1.0)
        out_h[pl.ds(t, 1), :] = jnp.where(living, -SLOPE * warm / rho, 0.0)

    paired_loop(stage, work, close, FORCE_BATCH)


SMEM = pl.BlockSpec(memory_space=pltpu.SMEM)
VMEM = pl.BlockSpec(memory_space=pltpu.VMEM)


DENSITY_BATCH = 4
FORCE_BATCH = 2


def density_call(rows, codes, state, place, weights):
    wide = (LANES, LINKS * LANES)
    return pl.pallas_call(
        density_kernel,
        out_shape=jax.ShapeDtypeStruct((SLOTS, LANES), F32),
        in_specs=[SMEM] * 2 + [VMEM] * 3,
        out_specs=VMEM,
        scratch_shapes=[
            pltpu.VMEM((SOURCES, 32, LANES), BF16),
            pltpu.VMEM((SLOTS, SHIFTED, LANES), BF16),
        ]
        + [pltpu.VMEM(wide, F32)] * (2 * DENSITY_BATCH)
        + [pltpu.VMEM((LANES, LANES), F32)] * (2 * DENSITY_BATCH),
        compiler_params=pltpu.CompilerParams(vmem_limit_bytes=32 << 20),
        name="density_pass",
    )(rows, codes, state, place, weights)


def force_call(rows, codes, state, rho_table, place, heat_place, weights, shift):
    tall = LINKS * LANES
    return pl.pallas_call(
        force_kernel,
        out_shape=(
            jax.ShapeDtypeStruct((3, SLOTS, LANES), F32),
            jax.ShapeDtypeStruct((SLOTS, LANES), F32),
        ),
        in_specs=[SMEM] * 2 + [VMEM] * 6,
        out_specs=(VMEM, VMEM),
        scratch_shapes=[
            pltpu.VMEM((SOURCES, 32, LANES), BF16),
            pltpu.VMEM((SOURCES, 32, LANES), BF16),
            pltpu.VMEM((SLOTS, 32, LANES), BF16),
            pltpu.VMEM((SOURCES, 16, LANES), BF16),
            pltpu.VMEM((SOURCES, LANES, LANES), F32),
            pltpu.VMEM((SLOTS, LANES), F32),
            pltpu.VMEM((SLOTS, SHIFTED, 2 * LANES), BF16),
            pltpu.VMEM((SLOTS, STILL, 2 * LANES), BF16),
        ]
        + [pltpu.VMEM((tall, 2 * LANES), F32)] * (2 * FORCE_BATCH)
        + [pltpu.VMEM((tall, 2 * LANES), F32)] * (2 * FORCE_BATCH)
        + [pltpu.VMEM((2 * tall, LANES), BF16)] * (2 * FORCE_BATCH)
        + [pltpu.VMEM((8, LANES), F32)] * (2 * FORCE_BATCH),
        compiler_params=pltpu.CompilerParams(vmem_limit_bytes=48 << 20),
        name="force_pass",
    )(rows, codes, state, rho_table, place, heat_place, weights, shift)


def padded(shard, axis, dim):
    size, here = lax.axis_size(axis), lax.axis_index(axis)
    even = lax.ppermute(shard, axis, [(i, i ^ 1) for i in range(size)])
    odd = lax.ppermute(shard, axis, [(i, (((i - 1) ^ 1) + 1) % size if i else size - 1) for i in range(size)])
    odd = jnp.where((here == 0) | (here == size - 1), 0.0, odd)
    lower = here % 2 == 0
    before, after = jnp.where(lower, odd, even), jnp.where(lower, even, odd)
    return jnp.concatenate([before, shard, after], axis=dim)


def halo(shard):
    return padded(padded(shard[None, None], "gx", 0), "gy", 1)


def eight_around(haloed):
    flat = haloed.reshape((9,) + haloed.shape[2:])
    picked = jnp.concatenate([flat[:4], flat[5:]], 0)
    return picked.reshape((8 * haloed.shape[2],) + haloed.shape[3:])


def owner(x, core, z, y):
    return (2 * x + core) * N_GY + 4 * z + y


CHIPS = [(x, c, z, y) for x in range(4) for c in range(2) for z in range(4) for y in range(4)]
STAGES = (
    [(0, 0, k, 0) for k in (1, 2, 3)],
    [(0, 0, 0, k) for k in (1, 2, 3)],
    [(k, 0, 0, 0) for k in (1, 2, 3)],
    [(0, 1, 0, 0)],
)


def gather_stage(shard, stage):
    pieces = [shard]
    for dx, dc, dz, dy in STAGES[stage]:
        pairs = [(owner(x, c, z, y), owner(x ^ dx, c ^ dc, z ^ dz, y ^ dy)) for x, c, z, y in CHIPS]
        pieces.append(lax.ppermute(shard, ("gx", "gy"), pairs))
    return jnp.concatenate(pieces, 0)


def exchange(leaving, edge):
    leaving = gather_stage(leaving, 0)
    leaving, edge = lax.optimization_barrier((leaving, edge[None, None]))
    leaving, edge = lax.optimization_barrier((gather_stage(leaving, 1), padded(edge, "gx", 0)))
    leaving, edge = lax.optimization_barrier((gather_stage(leaving, 2), padded(edge, "gy", 1)))
    return gather_stage(leaving, 3), edge


def place_of(gx, gy):
    number = jnp.arange(N_GX * N_GY * MIG)
    ox, oy = number // (MIG * N_GY), number // MIG % N_GY
    core = gx % 2 ^ ox % 2
    x = gx // 2 ^ ox // 2
    z = gy // 4 ^ oy // 4
    y = gy % 4 ^ oy % 4
    return (((core * 4 + x) * 4 + y) * 4 + z) * MIG + number % MIG


def local(
    cell_local_coords,
    particle_speeds,
    thermal_state,
    particle_weights,
    boundary_flag,
    departing_local_groups,
    migrant_target_holder,
    target_entry_inputs,
    adjacent_cell_label,
):
    gx, gy = lax.axis_index("gx"), lax.axis_index("gy")
    state_tables = jnp.concatenate(
        [
            cell_local_coords.transpose(1, 0, 2),
            particle_speeds.transpose(1, 0, 2),
            thermal_state[None],
            particle_weights[None],
            boundary_flag.astype(jnp.float32)[None],
        ],
        0,
    )
    width, blocks, lanes = state_tables.shape
    chosen = departing_local_groups[0]
    leaving = jnp.take(state_tables, chosen, axis=1).transpose(1, 0, 2)
    departed = jnp.any(jnp.arange(blocks)[:, None] == chosen[None, :], 1)
    staying = jnp.where(departed[None, :, None], 0.0, state_tables)
    edge = BND - IN_CAP
    incoming, haloed = exchange(leaving.reshape(MIG * width, lanes), staying[:, :edge].reshape(width * edge, lanes))
    around = haloed.reshape((9, width, edge, lanes))
    near_x = gx + jnp.array([-1, -1, -1, 0, 0, 0, 1, 1, 1])
    near_y = gy + jnp.array([-1, 0, 1, -1, 0, 1, -1, 0, 1])
    inside = (near_x >= 0) & (near_x < N_GX) & (near_y >= 0) & (near_y < N_GY)
    match = migrant_target_holder.reshape(-1)[None, :] == (near_x * N_GY + near_y)[:, None]
    match = match & inside[:, None]
    ranking = jnp.cumsum(match.astype(jnp.int32), axis=1) - 1
    taken = match[:, None, :] & (ranking[:, None, :] == jnp.arange(IN_CAP)[None, :, None])
    places = place_of(gx, gy)
    wanted = jnp.sum(jnp.where(taken, places[None, None, :], 0), 2)
    present = jnp.any(taken, 2)
    incoming = incoming.reshape(-1, width, lanes)
    arrived = jnp.where(present[:, :, None, None], jnp.take(incoming, wanted, axis=0), 0.0).transpose(0, 2, 1, 3)
    first = jnp.concatenate([arrived, around], 2)
    ghosts = [first[q] for q in range(9) if q != 4]
    state = jnp.concatenate([arrived[4], staying, *ghosts], 1)
    rows = target_entry_inputs.reshape(-1)
    codes = (adjacent_cell_label + (adjacent_cell_label >= 13).astype(jnp.int32)).reshape(-1)
    square, closing, weights, shift = pair_rows()
    square, closing, weights, heat_place = (jnp.asarray(a, BF16) for a in (square, closing, weights, heat_rows()))
    place = jnp.concatenate([square, closing], 0)
    density = density_call(rows, codes, state, square, weights)
    again = eight_around(halo(density[:BND]))
    rho_table = jnp.concatenate([density, again], 0)
    acceleration, heating = force_call(
        rows, codes, state, rho_table, place, heat_place, weights, jnp.asarray(shift)
    )
    return density, acceleration.transpose(1, 0, 2), heating


def solution(mesh):
    return jax.shard_map(
        local,
        mesh=mesh,
        in_specs=(
            P(("gx", "gy"), None, None),
            P(("gx", "gy"), None, None),
            P(("gx", "gy"), None),
            P(("gx", "gy"), None),
            P(("gx", "gy"), None),
            P(("gx", "gy"), None),
            P(),
            P(("gx", "gy"), None),
            P(("gx", "gy"), None),
        ),
        out_specs=(P(("gx", "gy"), None), P(("gx", "gy"), None, None), P(("gx", "gy"), None)),
        check_vma=False,
    )
```

```python
import functools
import math

import jax
import jax.numpy as jnp
import numpy as np
from jax import lax
from jax.experimental import pallas as pl
from jax.experimental.pallas import tpu as pltpu
from jax.sharding import PartitionSpec as P

IN_CAP = 8
BND = 16
MIG = 2
N_GX = 8
N_GY = 16
SLOTS = 104
SOURCES = 232
LANES = 128
LINKS = 9

SMOOTH = 0.5
KERNEL = 21.0 / (16.0 * math.pi * SMOOTH**3)
SOUND = math.sqrt(7.0)
VISC = 0.1
SOFT = 0.01 * SMOOTH**2
GRAVITY = 1.0
KAPPA = -2.0 * VISC * SOUND * SMOOTH
SLOPE = 5.0 * KERNEL / SMOOTH**2
TINY = 1e-30

F32 = jnp.float32
BF16 = jnp.bfloat16

PARTS = ((0, 0), (0, 1), (0, 2), (1, 0), (1, 1), (2, 0))
ONE = 24
STILL = 64
SHIFTED = 112


def part(p, channel):
    return 8 * p + channel


def source_at(p_target, p_source, channel):
    return 48 + channel if p_source == 2 else 16 * p_target + 8 * p_source + channel


def pair_rows():
    square = np.zeros((SHIFTED, 32), np.float32)
    closing = np.zeros((SHIFTED, 32), np.float32)
    steps = np.array([(c // 9 - 1, c // 3 % 3 - 1, c % 3 - 1) for c in range(27)], np.float32)
    weights = np.zeros((32, SHIFTED - STILL), np.float32)
    for k in range(3):
        for a, b in PARTS:
            square[source_at(a, b, k), part(a, k)] = -2
            closing[source_at(a, b, k), part(a, 3 + k)] = -1
            closing[source_at(a, b, 3 + k), part(a, k)] = -1
        for p in range(3):
            row = 64 + 8 * p
            square[row + k, ONE] = 2
            closing[row + 3 + k, ONE] = 1
            weights[:27, 8 * p + k] = weights[:27, 8 * p + 3 + k] = steps[:, k]
            row = (88, 96, 99)[p] + k
            square[row, part(p, k)] = -2
            closing[row, part(p, 3 + k)] = -1
            weights[:27, row - 64] = steps[:, k]
    for p in range(3):
        square[source_at(0, p, 6), ONE] = 1
        square[56 + p, part(p, 6)] = 1
        closing[source_at(0, p, 7), ONE] = 1
        closing[56 + p, part(p, 7)] = 1
    square[91, ONE] = 1
    weights[:27, 91 - 64] = (steps * steps).sum(1)
    shift = np.zeros((32, 8, LANES), np.float32)
    shift[:27, :3] = steps[:, :, None]
    weights = np.broadcast_to(weights[:, :, None], weights.shape + (LANES,))
    return square, closing, weights, shift


def heat_rows():
    heat, rho = (np.zeros((STILL, 32), np.float32) for _ in range(2))
    for a, b in PARTS:
        heat[source_at(a, b, 0), part(a, 0)] = 1
        heat[source_at(a, b, 1), part(a, 1)] = 1
    for p in range(3):
        heat[source_at(0, p, 2), ONE] = -1
        heat[source_at(0, p, 3), part(0, 2)] = -1
        rho[source_at(0, p, 4), ONE] = 1
        rho[56 + p, part(p, 3)] = 1
    return np.concatenate([heat, rho])


def split(block):
    high = block.astype(BF16).astype(F32)
    rest = block - high
    middle = rest.astype(BF16).astype(F32)
    return high, middle, rest - middle


def parts_of(block):
    return jnp.concatenate([*split(block), jnp.ones_like(block)], 0).astype(BF16)


def stacked(parts, row, lanes_weights=None, ones=False):
    first, second = parts[row, 0:16, :], parts[row, 16:32, :]
    rows = [first, first, first, second]
    if ones:
        more = [first, second, jnp.ones_like(first)]
        if lanes_weights is not None:
            more = [lanes_weights[16 * q : 16 * q + 16, :] * tile for q, tile in enumerate(more)]
        rows += more
    return jnp.concatenate(rows, 0)


def line(state, channel, b):
    return state[channel, pl.ds(b, 1), :]


def channels(state, b):
    x = [line(state, k, b) for k in range(3)]
    v = [line(state, 3 + k, b) * KAPPA for k in range(3)]
    n = x[0] * x[0] + x[1] * x[1] + x[2] * x[2]
    vx = x[0] * v[0] + x[1] * v[1] + x[2] * v[2]
    return jnp.concatenate([*x, *v, n, vx], 0)


def dot(a, b, contract):
    return lax.dot_general(a, b, (contract, ((), ())), preferred_element_type=F32)


def build_targets(place, parts, out, rows, first, count):
    for u in range(count // 2):
        at = first + 2 * u
        both = jnp.concatenate([parts[at], parts[at + 1]], 1)
        got = dot(place[...], both, ((1,), (0,))).astype(BF16)
        for q in range(2):
            for g in range(got.shape[0] // rows):
                out[at + q, :, LANES * g : LANES * (g + 1)] = got[rows * g : rows * (g + 1), LANES * q : LANES * (q + 1)]


def build_tables(own, other, targets):
    def first(u, carry):
        for q in range(26):
            own(26 * u + q)
        targets(26 * u, 26)
        return carry

    def second(u, carry):
        for q in range(32):
            other(SLOTS + 32 * u + q)
        return carry

    lax.fori_loop(0, SLOTS // 26, first, 0)
    lax.fori_loop(0, (SOURCES - SLOTS) // 32, second, 0)


def source_row(rows, t, k):
    return t if k == 0 else rows[t * 8 + k - 1]


def run(steps):
    for _ in steps:
        pass


def alternate(*steps):
    live = list(steps)
    while live:
        for g in list(live):
            if next(g, live) is live:
                live.remove(g)


def paired_loop(stage, work, close, batch):
    last = SLOTS // batch - 1
    span = lambda n: [n * batch + q for q in range(batch)]

    def chain(piece, n, slot):
        for q, t in enumerate(span(n)):
            yield from piece(t, slot * batch + q)

    run(chain(stage, 0, 0))

    def step(n, carry):
        for slot in range(2):

            @pl.when(lax.rem(n, 2) == slot)
            def _():
                alternate(
                    chain(close, jnp.maximum(n - 1, 0), 1 - slot),
                    chain(work, n, slot),
                    chain(stage, jnp.minimum(n + 1, last), 1 - slot),
                )

        return carry

    lax.fori_loop(0, last + 1, step, 0)
    run(chain(close, last, last % 2))


GROUPS = ((0, 1), (2, 3), (4,), (5, 6), (7, 8))


def fill_state(wanted, staying, around, incoming, state):
    width = state.shape[0]

    def owner_slots(q, first):
        for s in range(IN_CAP):
            place = wanted[IN_CAP * q + s]
            for c in range(width):
                found = incoming[pl.ds(jnp.maximum(place, 0) * width + c, 1), :]
                state[c, first + s : first + s + 1, :] = jnp.where(place >= 0, found, 0.0)

    for c in range(width):
        state[c, IN_CAP:SLOTS, :] = staying[c]
    owner_slots(4, 0)
    for at, q in enumerate((0, 1, 2, 3, 5, 6, 7, 8)):
        first = SLOTS + BND * at
        owner_slots(q, first)
        for c in range(width):
            state[c, first + IN_CAP : first + BND, :] = around[q, c]


def density_kernel(rows, codes, wanted, staying, around, incoming, place, weights, out, state, parts, left, *buffers):
    fill_state(wanted, staying, around, incoming, state)
    squares, sums = buffers[: 2 * DENSITY_BATCH], buffers[2 * DENSITY_BATCH :]

    def each(b):
        parts[b] = parts_of(channels(state, b))

    build_tables(each, each, lambda t, count: build_targets(place, parts, left, SHIFTED, t, count))

    def stage(t, slot):
        near, far = left[t, 0:STILL, :], left[t]
        for group in GROUPS:
            face = group[0] >= 5
            columns = [
                stacked(parts, source_row(rows, t, k), weights[codes[t * 4 + k - 5]] if face else None, face)
                for k in group
            ]
            sources = columns[0] if len(columns) == 1 else jnp.concatenate(columns, 1)
            made = dot(far if face else near, sources, ((0,), (0,)))
            squares[slot][:, LANES * group[0] : LANES * (group[-1] + 1)] = made
            yield

    def work(t, slot):
        square = squares[slot]
        row = [source_row(rows, t, k) for k in range(LINKS)]
        for o in range(16):
            total = None
            for k in range(LINKS):
                s = jnp.maximum(square[8 * o : 8 * o + 8, LANES * k : LANES * (k + 1)], TINY)
                w = jnp.maximum(1.0 - s * lax.rsqrt(s), 0.0)
                w2 = w * w
                term = (w2 * w2) * (1.25 - w) * line(state, 7, row[k])
                total = term if total is None else total + term
            sums[slot][8 * o : 8 * o + 8, :] = total
            if o % 3 == 0:
                yield

    def close(t, slot):
        rho = jnp.sum(sums[slot][...].T, 0, keepdims=True) * (4.0 * KERNEL)
        out[pl.ds(t, 1), :] = jnp.where(line(state, 7, t) > 0.0, rho, 0.0)
        yield

    paired_loop(stage, work, close, DENSITY_BATCH)


def force_kernel(rows, codes, state, rho_table, place, heat_place, weights, shift, out_a, out_h,
                 parts, heat_parts, own_parts, mass_parts, pressures, own_pressure, left, heat_left, *buffers):
    pairs, heats, split_terms, heat_sums = (buffers[2 * FORCE_BATCH * q : 2 * FORCE_BATCH * (q + 1)] for q in range(4))

    row = lax.broadcasted_iota(jnp.int32, (32, LANES), 0)
    pick = jnp.where((row % 8 == 5) & (row < 24), 1.0, 0.0).astype(BF16)

    def each(b, b_own=False):
        parts[b] = parts_of(channels(state, b))
        heat, mass, wall = (line(state, channel, b) for channel in (6, 7, 8))
        rho = jnp.where(mass > 0.0, rho_table[pl.ds(b, 1), :], 1.0)
        inverse = 1.0 / rho
        r2 = rho * rho
        pressure = (r2 * r2 * r2 * rho - 1.0) * (inverse * inverse)
        ratio = mass * inverse
        a = ratio * (2.0 + 1.2 * wall)
        b2 = ratio * (1.2 + 3.6 * wall)
        zero = jnp.zeros_like(rho)
        heat_parts[b] = parts_of(jnp.concatenate([a, b2, a * heat, b2 * heat, rho, pressure, zero, zero], 0))
        if b_own:
            pressures[b] = jnp.broadcast_to(pressure, (LANES, LANES)).T
        else:
            pressures[b] = dot(heat_parts[b], pick, ((0,), (0,)))
        high, middle, low = split(
            jnp.concatenate([mass, *(mass * line(state, k, b) for k in range(3)), zero, zero, zero, zero], 0)
        )
        mass_parts[b] = jnp.concatenate([high[0:4], middle[0:4], low], 0).astype(BF16)
        return [heat, heat * wall, wall, rho, zero, zero, zero, zero], pressure

    def own(b):
        lines, pressure = each(b, True)
        own_parts[b] = parts_of(jnp.concatenate(lines, 0))
        own_pressure[pl.ds(b, 1), :] = pressure

    def targets(t, count):
        build_targets(place, parts, left, SHIFTED, t, count)
        build_targets(heat_place, own_parts, heat_left, STILL, t, count)

    build_tables(own, each, targets)

    def stage(t, slot):
        near, heat_near = left[t, 0:STILL, :], heat_left[t]
        for k in range(LINKS):
            row = source_row(rows, t, k)
            if k < 5:
                targets = near
            else:
                scale = weights[codes[t * 4 + k - 5]]
                targets = jnp.concatenate(
                    [near, left[t, STILL:SHIFTED, :] * jnp.concatenate([scale, scale], 1)], 0
                )
            block = slice(LANES * k, LANES * (k + 1))
            pairs[slot][block, :] = dot(stacked(parts, row, None, k >= 5), targets, ((0,), (0,)))
            heats[slot][block, :] = dot(stacked(heat_parts, row), heat_near, ((0,), (0,)))
            yield

    def work(t, slot):
        pair, heat, terms = pairs[slot], heats[slot], split_terms[slot]
        totals = [None] * 2
        pressure = own_pressure[pl.ds(t, 1), :]
        for k in range(LINKS):
            near = pressures.at[source_row(rows, t, k)]
            for o in range(8):
                found = []
                for q in range(2):
                    eight = slice(LANES * k + 16 * o + 8 * q, LANES * k + 16 * o + 8 * q + 8)
                    s = jnp.maximum(pair[eight, 0:LANES], TINY)
                    w = jnp.maximum(1.0 - s * lax.rsqrt(s), 0.0)
                    w3 = w * w * w
                    z = w3 * pl.reciprocal(s + SOFT, approx=True)
                    closing = jnp.maximum(pair[eight, LANES : 2 * LANES], 0.0)
                    viscous = closing * pl.reciprocal(heat[eight, LANES : 2 * LANES], approx=True)
                    sum_p = pressure + near[16 * o + 8 * q : 16 * o + 8 * q + 8, :]
                    found.append(sum_p * w3 + viscous * z)
                    warm = (s * z) * heat[eight, 0:LANES]
                    totals[q] = warm if totals[q] is None else totals[q] + warm
                term = jnp.concatenate(found, 0)
                high = term.astype(BF16)
                at = 2 * LANES * k + 16 * o
                terms[at : at + 16, :] = high
                terms[at + LANES : at + LANES + 16, :] = (term - high.astype(F32)).astype(BF16)
            yield
        heat_sums[slot][...] = totals[0] + totals[1]

    def close(t, slot):
        total, moved = None, [None] * 3
        for k in range(LINKS):
            mass = mass_parts[source_row(rows, t, k)]
            got = dot(
                jnp.concatenate([mass, mass], 1),
                split_terms[slot][2 * LANES * k : 2 * LANES * (k + 1), :],
                ((1,), (0,)),
            )
            total = got if total is None else total + got
            if k >= 5:
                pull = got[0:1] + got[4:5] + got[8:9]
                code = codes[t * 4 + k - 5]
                for axis in range(3):
                    more = shift[code, axis : axis + 1, :] * pull
                    moved[axis] = more if moved[axis] is None else moved[axis] + more
            yield
        total = total[0:4] + total[4:8] + total[8:12]
        mass, fluid = line(state, 7, t), 1.0 - line(state, 8, t)
        living = mass > 0.0
        for k in range(3):
            push = SLOPE * (line(state, k, t) * total[0:1] - (total[1 + k : 2 + k] + moved[k]))
            if k == 2:
                push = push - GRAVITY
            out_a[k, pl.ds(t, 1), :] = jnp.where(living, push * fluid, 0.0)
        warm = jnp.sum(heat_sums[slot][...], 0, keepdims=True)
        rho = jnp.where(living, rho_table[pl.ds(t, 1), :], 1.0)
        out_h[pl.ds(t, 1), :] = jnp.where(living, -SLOPE * warm / rho, 0.0)

    paired_loop(stage, work, close, FORCE_BATCH)


SMEM = pl.BlockSpec(memory_space=pltpu.SMEM)
VMEM = pl.BlockSpec(memory_space=pltpu.VMEM)


DENSITY_BATCH = 4
FORCE_BATCH = 2


def density_call(rows, codes, wanted, staying, around, incoming, place, weights):
    wide = (LANES, LINKS * LANES)
    return pl.pallas_call(
        density_kernel,
        out_shape=(
            jax.ShapeDtypeStruct((SLOTS, LANES), F32),
            jax.ShapeDtypeStruct((staying.shape[0], SOURCES, LANES), F32),
        ),
        in_specs=[SMEM] * 3 + [VMEM] * 5,
        out_specs=(VMEM, VMEM),
        scratch_shapes=[
            pltpu.VMEM((SOURCES, 32, LANES), BF16),
            pltpu.VMEM((SLOTS, SHIFTED, LANES), BF16),
        ]
        + [pltpu.VMEM(wide, F32)] * (2 * DENSITY_BATCH)
        + [pltpu.VMEM((LANES, LANES), F32)] * (2 * DENSITY_BATCH),
        compiler_params=pltpu.CompilerParams(vmem_limit_bytes=32 << 20),
        name="density_pass",
    )(rows, codes, wanted, staying, around, incoming, place, weights)


def force_call(rows, codes, state, rho_table, place, heat_place, weights, shift):
    tall = LINKS * LANES
    return pl.pallas_call(
        force_kernel,
        out_shape=(
            jax.ShapeDtypeStruct((3, SLOTS, LANES), F32),
            jax.ShapeDtypeStruct((SLOTS, LANES), F32),
        ),
        in_specs=[SMEM] * 2 + [VMEM] * 6,
        out_specs=(VMEM, VMEM),
        scratch_shapes=[
            pltpu.VMEM((SOURCES, 32, LANES), BF16),
            pltpu.VMEM((SOURCES, 32, LANES), BF16),
            pltpu.VMEM((SLOTS, 32, LANES), BF16),
            pltpu.VMEM((SOURCES, 16, LANES), BF16),
            pltpu.VMEM((SOURCES, LANES, LANES), F32),
            pltpu.VMEM((SLOTS, LANES), F32),
            pltpu.VMEM((SLOTS, SHIFTED, 2 * LANES), BF16),
            pltpu.VMEM((SLOTS, STILL, 2 * LANES), BF16),
        ]
        + [pltpu.VMEM((tall, 2 * LANES), F32)] * (2 * FORCE_BATCH)
        + [pltpu.VMEM((tall, 2 * LANES), F32)] * (2 * FORCE_BATCH)
        + [pltpu.VMEM((2 * tall, LANES), BF16)] * (2 * FORCE_BATCH)
        + [pltpu.VMEM((8, LANES), F32)] * (2 * FORCE_BATCH),
        compiler_params=pltpu.CompilerParams(vmem_limit_bytes=48 << 20),
        name="force_pass",
    )(rows, codes, state, rho_table, place, heat_place, weights, shift)


def padded(shard, axis, dim):
    size, here = lax.axis_size(axis), lax.axis_index(axis)
    even = lax.ppermute(shard, axis, [(i, i ^ 1) for i in range(size)])
    odd = lax.ppermute(shard, axis, [(i, (((i - 1) ^ 1) + 1) % size if i else size - 1) for i in range(size)])
    odd = jnp.where((here == 0) | (here == size - 1), 0.0, odd)
    lower = here % 2 == 0
    before, after = jnp.where(lower, odd, even), jnp.where(lower, even, odd)
    return jnp.concatenate([before, shard, after], axis=dim)


def halo(shard):
    return padded(padded(shard[None, None], "gx", 0), "gy", 1)


def eight_around(haloed):
    flat = haloed.reshape((9,) + haloed.shape[2:])
    picked = jnp.concatenate([flat[:4], flat[5:]], 0)
    return picked.reshape((8 * haloed.shape[2],) + haloed.shape[3:])


def owner(x, core, z, y):
    return (2 * x + core) * N_GY + 4 * z + y


CHIPS = [(x, c, z, y) for x in range(4) for c in range(2) for z in range(4) for y in range(4)]
STAGES = (
    [(0, 0, k, 0) for k in (1, 2, 3)],
    [(0, 0, 0, k) for k in (1, 2, 3)],
    [(k, 0, 0, 0) for k in (1, 2, 3)],
    [(0, 1, 0, 0)],
)


def gather_stage(shard, stage):
    pieces = [shard]
    for dx, dc, dz, dy in STAGES[stage]:
        pairs = [(owner(x, c, z, y), owner(x ^ dx, c ^ dc, z ^ dz, y ^ dy)) for x, c, z, y in CHIPS]
        pieces.append(lax.ppermute(shard, ("gx", "gy"), pairs))
    return jnp.concatenate(pieces, 0)


def exchange(leaving, edge):
    leaving = gather_stage(leaving, 0)
    leaving, edge = lax.optimization_barrier((leaving, edge[None, None]))
    leaving, edge = lax.optimization_barrier((gather_stage(leaving, 1), padded(edge, "gx", 0)))
    leaving, edge = lax.optimization_barrier((gather_stage(leaving, 2), padded(edge, "gy", 1)))
    return gather_stage(leaving, 3), edge


def place_of(gx, gy):
    number = jnp.arange(N_GX * N_GY * MIG)
    ox, oy = number // (MIG * N_GY), number // MIG % N_GY
    core = gx % 2 ^ ox % 2
    x = gx // 2 ^ ox // 2
    z = gy // 4 ^ oy // 4
    y = gy % 4 ^ oy % 4
    return (((core * 4 + x) * 4 + y) * 4 + z) * MIG + number % MIG


def local(
    cell_local_coords,
    particle_speeds,
    thermal_state,
    particle_weights,
    boundary_flag,
    departing_local_groups,
    migrant_target_holder,
    target_entry_inputs,
    adjacent_cell_label,
):
    gx, gy = lax.axis_index("gx"), lax.axis_index("gy")
    state_tables = jnp.concatenate(
        [
            cell_local_coords.transpose(1, 0, 2),
            particle_speeds.transpose(1, 0, 2),
            thermal_state[None],
            particle_weights[None],
            boundary_flag.astype(jnp.float32)[None],
        ],
        0,
    )
    width, blocks, lanes = state_tables.shape
    chosen = departing_local_groups[0]
    leaving = jnp.take(state_tables, chosen, axis=1).transpose(1, 0, 2)
    departed = jnp.any(jnp.arange(blocks)[:, None] == chosen[None, :], 1)
    staying = jnp.where(departed[None, :, None], 0.0, state_tables)
    edge = BND - IN_CAP
    incoming, haloed = exchange(leaving.reshape(MIG * width, lanes), staying[:, :edge].reshape(width * edge, lanes))
    around = haloed.reshape((9, width, edge, lanes))
    near_x = gx + jnp.array([-1, -1, -1, 0, 0, 0, 1, 1, 1])
    near_y = gy + jnp.array([-1, 0, 1, -1, 0, 1, -1, 0, 1])
    inside = (near_x >= 0) & (near_x < N_GX) & (near_y >= 0) & (near_y < N_GY)
    match = migrant_target_holder.reshape(-1)[None, :] == (near_x * N_GY + near_y)[:, None]
    match = match & inside[:, None]
    ranking = jnp.cumsum(match.astype(jnp.int32), axis=1) - 1
    taken = match[:, None, :] & (ranking[:, None, :] == jnp.arange(IN_CAP)[None, :, None])
    places = place_of(gx, gy)
    wanted = jnp.sum(jnp.where(taken, places[None, None, :], 0), 2)
    present = jnp.any(taken, 2)
    wanted = jnp.where(present, wanted, -1).reshape(-1)
    rows = target_entry_inputs.reshape(-1)
    codes = (adjacent_cell_label + (adjacent_cell_label >= 13).astype(jnp.int32)).reshape(-1)
    square, closing, weights, shift = pair_rows()
    square, closing, weights, heat_place = (jnp.asarray(a, BF16) for a in (square, closing, weights, heat_rows()))
    place = jnp.concatenate([square, closing], 0)
    density, state = density_call(rows, codes, wanted, staying, around, incoming, square, weights)
    again = eight_around(halo(density[:BND]))
    rho_table = jnp.concatenate([density, again], 0)
    acceleration, heating = force_call(
        rows, codes, state, rho_table, place, heat_place, weights, jnp.asarray(shift)
    )
    return density, acceleration.transpose(1, 0, 2), heating


def solution(mesh):
    return jax.shard_map(
        local,
        mesh=mesh,
        in_specs=(
            P(("gx", "gy"), None, None),
            P(("gx", "gy"), None, None),
            P(("gx", "gy"), None),
            P(("gx", "gy"), None),
            P(("gx", "gy"), None),
            P(("gx", "gy"), None),
            P(),
            P(("gx", "gy"), None),
            P(("gx", "gy"), None),
        ),
        out_specs=(P(("gx", "gy"), None), P(("gx", "gy"), None, None), P(("gx", "gy"), None)),
        check_vma=False,
    )
```

```python
import functools
import math

import jax
import jax.numpy as jnp
import numpy as np
from jax import lax
from jax.experimental import pallas as pl
from jax.experimental.pallas import tpu as pltpu
from jax.sharding import PartitionSpec as P

IN_CAP = 8
BND = 16
MIG = 2
N_GX = 8
N_GY = 16
SLOTS = 104
SOURCES = 232
LANES = 128
LINKS = 9

SMOOTH = 0.5
KERNEL = 21.0 / (16.0 * math.pi * SMOOTH**3)
SOUND = math.sqrt(7.0)
VISC = 0.1
SOFT = 0.01 * SMOOTH**2
GRAVITY = 1.0
KAPPA = -2.0 * VISC * SOUND * SMOOTH
SLOPE = 5.0 * KERNEL / SMOOTH**2
TINY = 1e-30

F32 = jnp.float32
BF16 = jnp.bfloat16

PARTS = ((0, 0), (0, 1), (0, 2), (1, 0), (1, 1), (2, 0))
ONE = 24
STILL = 64
SHIFTED = 112


def part(p, channel):
    return 8 * p + channel


def source_at(p_target, p_source, channel):
    return 48 + channel if p_source == 2 else 16 * p_target + 8 * p_source + channel


def pair_rows():
    square = np.zeros((SHIFTED, 32), np.float32)
    closing = np.zeros((SHIFTED, 32), np.float32)
    steps = np.array([(c // 9 - 1, c // 3 % 3 - 1, c % 3 - 1) for c in range(27)], np.float32)
    weights = np.zeros((32, SHIFTED - STILL), np.float32)
    for k in range(3):
        for a, b in PARTS:
            square[source_at(a, b, k), part(a, k)] = -2
            closing[source_at(a, b, k), part(a, 3 + k)] = -1
            closing[source_at(a, b, 3 + k), part(a, k)] = -1
        for p in range(3):
            row = 64 + 8 * p
            square[row + k, ONE] = 2
            closing[row + 3 + k, ONE] = 1
            weights[:27, 8 * p + k] = weights[:27, 8 * p + 3 + k] = steps[:, k]
            row = (88, 96, 99)[p] + k
            square[row, part(p, k)] = -2
            closing[row, part(p, 3 + k)] = -1
            weights[:27, row - 64] = steps[:, k]
    for p in range(3):
        square[source_at(0, p, 6), ONE] = 1
        square[56 + p, part(p, 6)] = 1
        closing[source_at(0, p, 7), ONE] = 1
        closing[56 + p, part(p, 7)] = 1
    square[91, ONE] = 1
    weights[:27, 91 - 64] = (steps * steps).sum(1)
    shift = np.zeros((32, 8, LANES), np.float32)
    shift[:27, :3] = steps[:, :, None]
    weights = np.broadcast_to(weights[:, :, None], weights.shape + (LANES,))
    return square, closing, weights, shift


def heat_rows():
    heat, rho = (np.zeros((STILL, 32), np.float32) for _ in range(2))
    for a, b in PARTS:
        heat[source_at(a, b, 0), part(a, 0)] = 1
        heat[source_at(a, b, 1), part(a, 1)] = 1
    for p in range(3):
        heat[source_at(0, p, 2), ONE] = -1
        heat[source_at(0, p, 3), part(0, 2)] = -1
        rho[source_at(0, p, 4), ONE] = 1
        rho[56 + p, part(p, 3)] = 1
    return np.concatenate([heat, rho])


def split(block):
    high = block.astype(BF16).astype(F32)
    rest = block - high
    middle = rest.astype(BF16).astype(F32)
    return high, middle, rest - middle


def parts_of(block):
    return jnp.concatenate([*split(block), jnp.ones_like(block)], 0).astype(BF16)


def stacked(parts, row, lanes_weights=None, ones=False):
    first, second = parts[row, 0:16, :], parts[row, 16:32, :]
    rows = [first, first, first, second]
    if ones:
        more = [first, second, jnp.ones_like(first)]
        if lanes_weights is not None:
            more = [lanes_weights[16 * q : 16 * q + 16, :] * tile for q, tile in enumerate(more)]
        rows += more
    return jnp.concatenate(rows, 0)


def line(state, channel, b):
    return state[channel, pl.ds(b, 1), :]


def channels(state, b):
    x = [line(state, k, b) for k in range(3)]
    v = [line(state, 3 + k, b) * KAPPA for k in range(3)]
    n = x[0] * x[0] + x[1] * x[1] + x[2] * x[2]
    vx = x[0] * v[0] + x[1] * v[1] + x[2] * v[2]
    return jnp.concatenate([*x, *v, n, vx], 0)


def dot(a, b, contract):
    return lax.dot_general(a, b, (contract, ((), ())), preferred_element_type=F32)


def build_targets(place, parts, out, rows, first, count):
    for u in range(count // 2):
        at = first + 2 * u
        both = jnp.concatenate([parts[at], parts[at + 1]], 1)
        got = dot(place[...], both, ((1,), (0,))).astype(BF16)
        for q in range(2):
            for g in range(got.shape[0] // rows):
                out[at + q, :, LANES * g : LANES * (g + 1)] = got[rows * g : rows * (g + 1), LANES * q : LANES * (q + 1)]


def build_tables(own, other, targets):
    def first(u, carry):
        for q in range(26):
            own(26 * u + q)
        targets(26 * u, 26)
        return carry

    def second(u, carry):
        for q in range(32):
            other(SLOTS + 32 * u + q)
        return carry

    lax.fori_loop(0, SLOTS // 26, first, 0)
    lax.fori_loop(0, (SOURCES - SLOTS) // 32, second, 0)


def source_row(rows, t, k):
    return t if k == 0 else rows[t * 8 + k - 1]


def run(steps):
    for _ in steps:
        pass


def alternate(*steps):
    live = list(steps)
    while live:
        for g in list(live):
            if next(g, live) is live:
                live.remove(g)


def paired_loop(stage, work, close, batch):
    last = SLOTS // batch - 1
    span = lambda n: [n * batch + q for q in range(batch)]

    def chain(piece, n, slot):
        for q, t in enumerate(span(n)):
            yield from piece(t, slot * batch + q)

    run(chain(stage, 0, 0))

    def step(n, carry):
        for slot in range(2):

            @pl.when(lax.rem(n, 2) == slot)
            def _():
                alternate(
                    chain(close, jnp.maximum(n - 1, 0), 1 - slot),
                    chain(work, n, slot),
                    chain(stage, jnp.minimum(n + 1, last), 1 - slot),
                )

        return carry

    lax.fori_loop(0, last + 1, step, 0)
    run(chain(close, last, last % 2))


GROUPS = ((0, 1), (2, 3), (4,), (5, 6), (7, 8))


def fill_state(wanted, staying, around, incoming, state):
    width = state.shape[0]

    def owner_slots(q, first):
        for s in range(IN_CAP):
            place = wanted[IN_CAP * q + s]
            for c in range(width):
                found = incoming[pl.ds(jnp.maximum(place, 0) * width + c, 1), :]
                state[c, first + s : first + s + 1, :] = jnp.where(place >= 0, found, 0.0)

    for c in range(width):
        state[c, IN_CAP:SLOTS, :] = staying[c]
    owner_slots(4, 0)
    for at, q in enumerate((0, 1, 2, 3, 5, 6, 7, 8)):
        first = SLOTS + BND * at
        owner_slots(q, first)
        for c in range(width):
            state[c, first + IN_CAP : first + BND, :] = around[q, c]


def density_kernel(rows, codes, wanted, staying, around, incoming, place, weights, out, state, parts, left, *buffers):
    fill_state(wanted, staying, around, incoming, state)
    squares, sums = buffers[: 2 * DENSITY_BATCH], buffers[2 * DENSITY_BATCH :]

    def each(b):
        parts[b] = parts_of(channels(state, b))

    build_tables(each, each, lambda t, count: build_targets(place, parts, left, SHIFTED, t, count))

    def stage(t, slot):
        near, far = left[t, 0:STILL, :], left[t]
        for group in GROUPS:
            face = group[0] >= 5
            columns = [
                stacked(parts, source_row(rows, t, k), weights[codes[t * 4 + k - 5]] if face else None, face)
                for k in group
            ]
            sources = columns[0] if len(columns) == 1 else jnp.concatenate(columns, 1)
            made = dot(far if face else near, sources, ((0,), (0,)))
            squares[slot][:, LANES * group[0] : LANES * (group[-1] + 1)] = made
            yield

    def work(t, slot):
        square = squares[slot]
        row = [source_row(rows, t, k) for k in range(LINKS)]
        for o in range(16):
            total = None
            for k in range(LINKS):
                s = jnp.maximum(square[8 * o : 8 * o + 8, LANES * k : LANES * (k + 1)], TINY)
                w = jnp.maximum(1.0 - s * lax.rsqrt(s), 0.0)
                w2 = w * w
                term = (w2 * w2) * (1.25 - w) * line(state, 7, row[k])
                total = term if total is None else total + term
            sums[slot][8 * o : 8 * o + 8, :] = total
            if o % 3 == 0:
                yield

    def close(t, slot):
        rho = jnp.sum(sums[slot][...].T, 0, keepdims=True) * (4.0 * KERNEL)
        out[pl.ds(t, 1), :] = jnp.where(line(state, 7, t) > 0.0, rho, 0.0)
        yield

    paired_loop(stage, work, close, DENSITY_BATCH)


def force_kernel(rows, codes, state, rho_table, place, heat_place, weights, shift, out_a, out_h,
                 parts, heat_parts, own_parts, mass_parts, pressures, own_pressure, left, heat_left, *buffers):
    pairs, heats, split_terms, heat_sums = (buffers[2 * FORCE_BATCH * q : 2 * FORCE_BATCH * (q + 1)] for q in range(4))

    row = lax.broadcasted_iota(jnp.int32, (32, LANES), 0)
    pick = jnp.where((row % 8 == 5) & (row < 24), 1.0, 0.0).astype(BF16)

    def each(b, b_own=False):
        parts[b] = parts_of(channels(state, b))
        heat, mass, wall = (line(state, channel, b) for channel in (6, 7, 8))
        rho = jnp.where(mass > 0.0, rho_table[pl.ds(b, 1), :], 1.0)
        inverse = 1.0 / rho
        r2 = rho * rho
        pressure = (r2 * r2 * r2 * rho - 1.0) * (inverse * inverse)
        ratio = mass * inverse
        a = ratio * (2.0 + 1.2 * wall)
        b2 = ratio * (1.2 + 3.6 * wall)
        zero = jnp.zeros_like(rho)
        heat_parts[b] = parts_of(jnp.concatenate([a, b2, a * heat, b2 * heat, rho, pressure, zero, zero], 0))
        if b_own:
            pressures[b] = jnp.broadcast_to(pressure, (LANES, LANES)).T
        else:
            pressures[b] = dot(heat_parts[b], pick, ((0,), (0,)))
        high, middle, low = split(
            jnp.concatenate([mass, *(mass * line(state, k, b) for k in range(3)), zero, zero, zero, zero], 0)
        )
        mass_parts[b] = jnp.concatenate([high[0:4], middle[0:4], low], 0).astype(BF16)
        return [heat, heat * wall, wall, rho, zero, zero, zero, zero], pressure

    def own(b):
        lines, pressure = each(b, True)
        own_parts[b] = parts_of(jnp.concatenate(lines, 0))
        own_pressure[pl.ds(b, 1), :] = pressure

    def targets(t, count):
        build_targets(place, parts, left, SHIFTED, t, count)
        build_targets(heat_place, own_parts, heat_left, STILL, t, count)

    build_tables(own, each, targets)

    def stage(t, slot):
        near, heat_near = left[t, 0:STILL, :], heat_left[t]
        for k in range(LINKS):
            row = source_row(rows, t, k)
            if k < 5:
                targets = near
            else:
                scale = weights[codes[t * 4 + k - 5]]
                targets = jnp.concatenate(
                    [near, left[t, STILL:SHIFTED, :] * jnp.concatenate([scale, scale], 1)], 0
                )
            block = slice(LANES * k, LANES * (k + 1))
            pairs[slot][block, :] = dot(stacked(parts, row, None, k >= 5), targets, ((0,), (0,)))
            heats[slot][block, :] = dot(stacked(heat_parts, row), heat_near, ((0,), (0,)))
            yield

    def work(t, slot):
        pair, heat, terms = pairs[slot], heats[slot], split_terms[slot]
        totals = [None] * 2
        pressure = own_pressure[pl.ds(t, 1), :]
        for k in range(LINKS):
            near = pressures.at[source_row(rows, t, k)]
            for o in range(8):
                found = []
                for q in range(2):
                    eight = slice(LANES * k + 16 * o + 8 * q, LANES * k + 16 * o + 8 * q + 8)
                    s = jnp.maximum(pair[eight, 0:LANES], TINY)
                    w = jnp.maximum(1.0 - s * lax.rsqrt(s), 0.0)
                    w3 = w * w * w
                    z = w3 * pl.reciprocal(s + SOFT, approx=True)
                    closing = jnp.maximum(pair[eight, LANES : 2 * LANES], 0.0)
                    viscous = closing * pl.reciprocal(heat[eight, LANES : 2 * LANES], approx=True)
                    sum_p = pressure + near[16 * o + 8 * q : 16 * o + 8 * q + 8, :]
                    found.append(sum_p * w3 + viscous * z)
                    warm = (s * z) * heat[eight, 0:LANES]
                    totals[q] = warm if totals[q] is None else totals[q] + warm
                term = jnp.concatenate(found, 0)
                high = term.astype(BF16)
                at = 2 * LANES * k + 16 * o
                terms[at : at + 16, :] = high
                terms[at + LANES : at + LANES + 16, :] = (term - high.astype(F32)).astype(BF16)
            yield
        heat_sums[slot][...] = totals[0] + totals[1]

    def close(t, slot):
        total, moved = None, [None] * 3
        for k in range(LINKS):
            mass = mass_parts[source_row(rows, t, k)]
            got = dot(
                jnp.concatenate([mass, mass], 1),
                split_terms[slot][2 * LANES * k : 2 * LANES * (k + 1), :],
                ((1,), (0,)),
            )
            total = got if total is None else total + got
            if k >= 5:
                pull = got[0:1] + got[4:5] + got[8:9]
                code = codes[t * 4 + k - 5]
                for axis in range(3):
                    more = shift[code, axis : axis + 1, :] * pull
                    moved[axis] = more if moved[axis] is None else moved[axis] + more
            yield
        total = total[0:4] + total[4:8] + total[8:12]
        mass, fluid = line(state, 7, t), 1.0 - line(state, 8, t)
        living = mass > 0.0
        for k in range(3):
            push = SLOPE * (line(state, k, t) * total[0:1] - (total[1 + k : 2 + k] + moved[k]))
            if k == 2:
                push = push - GRAVITY
            out_a[k, pl.ds(t, 1), :] = jnp.where(living, push * fluid, 0.0)
        warm = jnp.sum(heat_sums[slot][...], 0, keepdims=True)
        rho = jnp.where(living, rho_table[pl.ds(t, 1), :], 1.0)
        out_h[pl.ds(t, 1), :] = jnp.where(living, -SLOPE * warm / rho, 0.0)

    paired_loop(stage, work, close, FORCE_BATCH)


SMEM = pl.BlockSpec(memory_space=pltpu.SMEM)
VMEM = pl.BlockSpec(memory_space=pltpu.VMEM)


DENSITY_BATCH = 4
FORCE_BATCH = 4


def density_call(rows, codes, wanted, staying, around, incoming, place, weights):
    wide = (LANES, LINKS * LANES)
    return pl.pallas_call(
        density_kernel,
        out_shape=(
            jax.ShapeDtypeStruct((SLOTS, LANES), F32),
            jax.ShapeDtypeStruct((staying.shape[0], SOURCES, LANES), F32),
        ),
        in_specs=[SMEM] * 3 + [VMEM] * 5,
        out_specs=(VMEM, VMEM),
        scratch_shapes=[
            pltpu.VMEM((SOURCES, 32, LANES), BF16),
            pltpu.VMEM((SLOTS, SHIFTED, LANES), BF16),
        ]
        + [pltpu.VMEM(wide, F32)] * (2 * DENSITY_BATCH)
        + [pltpu.VMEM((LANES, LANES), F32)] * (2 * DENSITY_BATCH),
        compiler_params=pltpu.CompilerParams(vmem_limit_bytes=32 << 20),
        name="density_pass",
    )(rows, codes, wanted, staying, around, incoming, place, weights)


def force_call(rows, codes, state, rho_table, place, heat_place, weights, shift):
    tall = LINKS * LANES
    return pl.pallas_call(
        force_kernel,
        out_shape=(
            jax.ShapeDtypeStruct((3, SLOTS, LANES), F32),
            jax.ShapeDtypeStruct((SLOTS, LANES), F32),
        ),
        in_specs=[SMEM] * 2 + [VMEM] * 6,
        out_specs=(VMEM, VMEM),
        scratch_shapes=[
            pltpu.VMEM((SOURCES, 32, LANES), BF16),
            pltpu.VMEM((SOURCES, 32, LANES), BF16),
            pltpu.VMEM((SLOTS, 32, LANES), BF16),
            pltpu.VMEM((SOURCES, 16, LANES), BF16),
            pltpu.VMEM((SOURCES, LANES, LANES), F32),
            pltpu.VMEM((SLOTS, LANES), F32),
            pltpu.VMEM((SLOTS, SHIFTED, 2 * LANES), BF16),
            pltpu.VMEM((SLOTS, STILL, 2 * LANES), BF16),
        ]
        + [pltpu.VMEM((tall, 2 * LANES), F32)] * (2 * FORCE_BATCH)
        + [pltpu.VMEM((tall, 2 * LANES), F32)] * (2 * FORCE_BATCH)
        + [pltpu.VMEM((2 * tall, LANES), BF16)] * (2 * FORCE_BATCH)
        + [pltpu.VMEM((8, LANES), F32)] * (2 * FORCE_BATCH),
        compiler_params=pltpu.CompilerParams(vmem_limit_bytes=60 << 20),
        name="force_pass",
    )(rows, codes, state, rho_table, place, heat_place, weights, shift)


def padded(shard, axis, dim):
    size, here = lax.axis_size(axis), lax.axis_index(axis)
    even = lax.ppermute(shard, axis, [(i, i ^ 1) for i in range(size)])
    odd = lax.ppermute(shard, axis, [(i, (((i - 1) ^ 1) + 1) % size if i else size - 1) for i in range(size)])
    odd = jnp.where((here == 0) | (here == size - 1), 0.0, odd)
    lower = here % 2 == 0
    before, after = jnp.where(lower, odd, even), jnp.where(lower, even, odd)
    return jnp.concatenate([before, shard, after], axis=dim)


def halo(shard):
    return padded(padded(shard[None, None], "gx", 0), "gy", 1)


def eight_around(haloed):
    flat = haloed.reshape((9,) + haloed.shape[2:])
    picked = jnp.concatenate([flat[:4], flat[5:]], 0)
    return picked.reshape((8 * haloed.shape[2],) + haloed.shape[3:])


def owner(x, core, z, y):
    return (2 * x + core) * N_GY + 4 * z + y


CHIPS = [(x, c, z, y) for x in range(4) for c in range(2) for z in range(4) for y in range(4)]
STAGES = (
    [(0, 0, k, 0) for k in (1, 2, 3)],
    [(0, 0, 0, k) for k in (1, 2, 3)],
    [(k, 0, 0, 0) for k in (1, 2, 3)],
    [(0, 1, 0, 0)],
)


def gather_stage(shard, stage):
    pieces = [shard]
    for dx, dc, dz, dy in STAGES[stage]:
        pairs = [(owner(x, c, z, y), owner(x ^ dx, c ^ dc, z ^ dz, y ^ dy)) for x, c, z, y in CHIPS]
        pieces.append(lax.ppermute(shard, ("gx", "gy"), pairs))
    return jnp.concatenate(pieces, 0)


def exchange(leaving, edge):
    leaving = gather_stage(leaving, 0)
    leaving, edge = lax.optimization_barrier((leaving, edge[None, None]))
    leaving, edge = lax.optimization_barrier((gather_stage(leaving, 1), padded(edge, "gx", 0)))
    leaving, edge = lax.optimization_barrier((gather_stage(leaving, 2), padded(edge, "gy", 1)))
    return gather_stage(leaving, 3), edge


def place_of(gx, gy):
    number = jnp.arange(N_GX * N_GY * MIG)
    ox, oy = number // (MIG * N_GY), number // MIG % N_GY
    core = gx % 2 ^ ox % 2
    x = gx // 2 ^ ox // 2
    z = gy // 4 ^ oy // 4
    y = gy % 4 ^ oy % 4
    return (((core * 4 + x) * 4 + y) * 4 + z) * MIG + number % MIG


def local(
    cell_local_coords,
    particle_speeds,
    thermal_state,
    particle_weights,
    boundary_flag,
    departing_local_groups,
    migrant_target_holder,
    target_entry_inputs,
    adjacent_cell_label,
):
    gx, gy = lax.axis_index("gx"), lax.axis_index("gy")
    state_tables = jnp.concatenate(
        [
            cell_local_coords.transpose(1, 0, 2),
            particle_speeds.transpose(1, 0, 2),
            thermal_state[None],
            particle_weights[None],
            boundary_flag.astype(jnp.float32)[None],
        ],
        0,
    )
    width, blocks, lanes = state_tables.shape
    chosen = departing_local_groups[0]
    leaving = jnp.take(state_tables, chosen, axis=1).transpose(1, 0, 2)
    departed = jnp.any(jnp.arange(blocks)[:, None] == chosen[None, :], 1)
    staying = jnp.where(departed[None, :, None], 0.0, state_tables)
    edge = BND - IN_CAP
    incoming, haloed = exchange(leaving.reshape(MIG * width, lanes), staying[:, :edge].reshape(width * edge, lanes))
    around = haloed.reshape((9, width, edge, lanes))
    near_x = gx + jnp.array([-1, -1, -1, 0, 0, 0, 1, 1, 1])
    near_y = gy + jnp.array([-1, 0, 1, -1, 0, 1, -1, 0, 1])
    inside = (near_x >= 0) & (near_x < N_GX) & (near_y >= 0) & (near_y < N_GY)
    match = migrant_target_holder.reshape(-1)[None, :] == (near_x * N_GY + near_y)[:, None]
    match = match & inside[:, None]
    ranking = jnp.cumsum(match.astype(jnp.int32), axis=1) - 1
    taken = match[:, None, :] & (ranking[:, None, :] == jnp.arange(IN_CAP)[None, :, None])
    places = place_of(gx, gy)
    wanted = jnp.sum(jnp.where(taken, places[None, None, :], 0), 2)
    present = jnp.any(taken, 2)
    wanted = jnp.where(present, wanted, -1).reshape(-1)
    rows = target_entry_inputs.reshape(-1)
    codes = (adjacent_cell_label + (adjacent_cell_label >= 13).astype(jnp.int32)).reshape(-1)
    square, closing, weights, shift = pair_rows()
    square, closing, weights, heat_place = (jnp.asarray(a, BF16) for a in (square, closing, weights, heat_rows()))
    place = jnp.concatenate([square, closing], 0)
    density, state = density_call(rows, codes, wanted, staying, around, incoming, square, weights)
    again = eight_around(halo(density[:BND]))
    rho_table = jnp.concatenate([density, again], 0)
    acceleration, heating = force_call(
        rows, codes, state, rho_table, place, heat_place, weights, jnp.asarray(shift)
    )
    return density, acceleration.transpose(1, 0, 2), heating


def solution(mesh):
    return jax.shard_map(
        local,
        mesh=mesh,
        in_specs=(
            P(("gx", "gy"), None, None),
            P(("gx", "gy"), None, None),
            P(("gx", "gy"), None),
            P(("gx", "gy"), None),
            P(("gx", "gy"), None),
            P(("gx", "gy"), None),
            P(),
            P(("gx", "gy"), None),
            P(("gx", "gy"), None),
        ),
        out_specs=(P(("gx", "gy"), None), P(("gx", "gy"), None, None), P(("gx", "gy"), None)),
        check_vma=False,
    )
```
